32 devices in a mesh: sect: 2 (over core), gy: 4 (over y, x), gx: 4 (over z).
Axes of the slice: x: 2, y: 2, z: 4, core: 2. Of those that a mesh axis runs over, the one named last changes fastest.
Arguments:
- adjoint_init: float32 [2, 32, 128, 1024], P('sect', None, 'gy', 'gx'), may hold values from -6 to 6
- diffusivity: float32 [2, 128, 1024], P('sect', 'gy', 'gx'), may hold values from 0.02 to 0.12
- mixing: float32 [2, 32, 32], P('sect'), may hold values from -0.75 to 0.75
- coupling: float32 [2, 32, 8], P('sect'), may hold values from -6 to 6
- history: float32 [2, 4, 4, 128, 1024], P('sect', None, None, 'gy', 'gx'), may hold values from -6 to 6
- extract: float32 [4, 32], replicated, may hold values from -3 to 3
- land_mask: int32 [128, 1024], P('gy', 'gx'), may hold values 0 or 1
- regrid: float32 [16, 128, 128], P(('gy', 'gx')), may hold values from -0.5 to 0.5
- atmos_tile_index: int32 [2048, 1], replicated, may hold values from 0 to 15; in each aligned block of 128 rows (0 to 127, 128 to 255, ...) at most 16 rows name the same one
- ocean_block_index: int32 [2048], replicated, may hold values from 0 to 63
- atmos_block_index: int32 [2048], replicated, may hold values from 0 to 63
Outputs:
- adjoint_state: float32 [2, 32, 128, 1024], P('sect', None, 'gy', 'gx')
The draws below stay inside these ranges and needn't reach their ends.
Inputs may be any that keep to these rules, and one draw needn't show every extreme that they name: `atmos_tile_index`: list rows i*128 to (i+1)*128 - 1 are ocean tile i's entries; among them at most 16 name the same atmosphere tile, and exactly 16 do so for some atmosphere tile.
All inputs are finite; a program needn't handle non-finite values. No bound on the sum of `land_mask` on one device may be relied on, other than what follows from the above.
Results may differ from the reference program's by a relative error of at most 0.0001.
Values sent between devices are 32-bit elements; how exact they have to be, the bound alone decides.
No kernel may reach another device: no remote copies, remote signals or barrier semaphores. Data moves between devices by JAX's collectives and lax.ppermute only.
A program may use at most 64 MiB of HBM per device.

```python
import math
import jax
import jax.numpy as jnp
import numpy as np
from jax import lax

COUPLING_FIELDS = 4
WINDOW_STEPS = 4
BLOCK_GRID_CELLS = 128
CY = 32
CX = 256
REGRID_ENTRIES = 128
NC = 32
SECTION_TILES = 16
CAP = 16
TILE_BLOCKS = 64
NY = 128
NX = 1024
N_GY = 4
N_GX = 4


def place_ends(entries, stream_key, low, high):
    longest = entries.shape.index(max(entries.shape))
    spots = []
    for shift in (0, 1):
        where = [jax.random.randint(jax.random.fold_in(stream_key, axis), (), 0, length) for axis, length in enumerate(entries.shape)]
        where[longest] = (where[longest] + shift) % entries.shape[longest]
        spots.append(tuple(where))
    return entries.at[spots[0]].set(low).at[spots[1]].set(high)


def levels(stream_key, extent, shards, smallest, top_value):
    def one(position, blocks):
        heights = jax.random.uniform(jax.random.fold_in(jax.random.fold_in(stream_key, 6), position), (blocks,), jnp.float32, smallest / len(shards), top_value / len(shards))
        return jnp.repeat(jnp.exp(heights), extent[position] // blocks).reshape((-1,) + (1,) * (len(extent) - position - 1))

    level = one(*shards[0])
    for cut in shards[1:]:
        level = level * one(*cut)
    return level


def deal_out(own_key, own, number, rows, count, top, bound, skew):
    order = jax.random.permutation(own_key, count)
    crowded, usual = portions_of(count, rows * top, bound, skew, True), portions_of(count, rows * top, bound, skew, False)
    places = jnp.arange(count)

    def named(tallies, rotation):
        used = int((tallies > 0).sum())
        fixed = max(1, used // 4)
        shifted = fixed + (places - fixed + rotation * (used - fixed)) % max(1, count - fixed)
        return jnp.zeros((count,), jnp.int32).at[order[jnp.where(places < fixed, places, shifted)]].set(jnp.asarray(tallies, jnp.int32))

    tallies = jnp.where(number % 4 == 0, named(crowded, number // 4), named(usual, number - number // 4 - 1))
    mixed = jax.random.permutation(jax.random.fold_in(own, 3), count)
    giver, taker = mixed[0:count // 2 * 2:2], mixed[1:count // 2 * 2:2]
    room = jnp.minimum(tallies[giver] - 1, bound - tallies[taker]) // 2
    room = jnp.where((giver == order[0]) | (taker == order[0]) | (tallies[taker] == 0), 0, jnp.maximum(room, 0))
    shifted = jax.random.randint(jax.random.fold_in(own, 4), (count // 2,), 0, 1 << 20) % (room + 1)
    tallies = tallies.at[giver].add(-shifted).at[taker].add(shifted)
    members = jnp.searchsorted(jnp.cumsum(tallies), jnp.arange(rows * top), side="right").astype(jnp.int32)
    grid = members.reshape(top, rows).T
    grid = grid[jax.random.permutation(jax.random.fold_in(own, 1), rows)]
    rotation = jax.random.randint(jax.random.fold_in(own, 2), (rows, 1), 0, top)
    return jnp.take_along_axis(grid, (jnp.arange(top)[None, :] + rotation) % top, axis=1)


def portions_of(number_of, total, bound, skew, full):
    loads = [(1 << 20) // math.isqrt(grade ** skew) + 1 for grade in range(1, number_of + 1)]
    largest = bound if full else min(bound, max(-(-total // number_of), total * loads[0] // sum(loads)))
    least = 1 if total - largest >= number_of - 1 else 0
    counts, surplus = [largest] + [least] * (number_of - 1), total - largest - least * (number_of - 1)
    while surplus > 0:
        movable = [i for i in range(1, number_of) if counts[i] < largest] or [i for i in range(1, number_of) if counts[i] < bound]
        pool, budget = sum([loads[i] for i in movable]), surplus
        for i in movable:
            more = min(bound - counts[i], max(1, budget * loads[i] // pool), surplus)
            counts[i] = counts[i] + more
            surplus = surplus - more
    return np.array(counts)


def noise(stream_key, dims, width, bound, split=(), kind=jnp.bfloat16):
    values = width * jax.random.normal(stream_key, dims, jnp.float32)
    if split:
        values = values * levels(stream_key, dims, split, -0.22, 0.18)
    return jnp.clip(values, -bound, bound).astype(kind)


def setup_inputs(seed: int = 0) -> dict:
    seeds = jax.random.split(jax.random.key(seed), 12)
    adjoint_init = noise(seeds[0], (2, NC, NY, NX), 1.0, 6.0, ((0, 2), (2, 4), (3, 4)), jnp.float32)
    diffusivity = jnp.clip(jnp.exp(math.log(0.12) - 1.7917595 * jax.random.uniform(seeds[1], (2, NY, NX), jnp.float32) ** levels(seeds[1], (2, NY, NX), ((0, 2), (1, 4), (2, 4)), -0.2, 0.2)), 0.02, 0.12)
    mixing = noise(seeds[2], (2, NC, NC), 0.05, 0.75, ((0, 2),), jnp.float32)
    coupling = noise(seeds[3], (2, NC, 2 * COUPLING_FIELDS), 0.5, 6.0, ((0, 2),), jnp.float32)
    history = noise(seeds[4], (2, WINDOW_STEPS, COUPLING_FIELDS, NY, NX), 1.0, 6.0, ((0, 2), (3, 4), (4, 4)), jnp.float32)
    extract = noise(seeds[5], (COUPLING_FIELDS, NC), 0.2, 3.0, (), jnp.float32)
    land_mask = place_ends((jax.random.randint(seeds[6], (NY, NX), 0, 4) < 3).astype(jnp.int32), jax.random.fold_in(seeds[6], 1), 0, 1)
    regrid = noise(seeds[7], (SECTION_TILES, BLOCK_GRID_CELLS, BLOCK_GRID_CELLS), BLOCK_GRID_CELLS ** -0.5, 0.5, ((0, 16),), jnp.float32)
    atmos_tile_index_keys = jax.random.split(jax.random.fold_in(seeds[8], 1), (SECTION_TILES * REGRID_ENTRIES) // REGRID_ENTRIES)
    atmos_tile_index_turns = jax.random.permutation(jax.random.fold_in(seeds[8], 3), (SECTION_TILES * REGRID_ENTRIES) // REGRID_ENTRIES)
    atmos_tile_index = jax.vmap(lambda own, number: deal_out(jax.random.fold_in(seeds[8], 2), own, number, REGRID_ENTRIES, SECTION_TILES, 1, CAP, 2))(atmos_tile_index_keys, atmos_tile_index_turns).reshape((SECTION_TILES * REGRID_ENTRIES, 1))
    ocean_block_index = place_ends(jax.random.randint(seeds[9], (SECTION_TILES * REGRID_ENTRIES,), 0, TILE_BLOCKS), jax.random.fold_in(seeds[9], 1), 0, TILE_BLOCKS - 1).astype(jnp.int32)
    atmos_block_index = place_ends(jax.random.randint(seeds[10], (SECTION_TILES * REGRID_ENTRIES,), 0, TILE_BLOCKS), jax.random.fold_in(seeds[10], 1), 0, TILE_BLOCKS - 1).astype(jnp.int32)
    return {"adjoint_init": adjoint_init, "diffusivity": diffusivity, "mixing": mixing, "coupling": coupling, "history": history, "extract": extract, "land_mask": land_mask, "regrid": regrid, "atmos_tile_index": atmos_tile_index, "ocean_block_index": ocean_block_index, "atmos_block_index": atmos_block_index}


def laplace(field):
    padded = jnp.pad(field, ((0, 0), (1, 1), (0, 0)))
    return (padded[:, 2:, :] + padded[:, :-2, :] + jnp.roll(field, 1, axis=2)
            + jnp.roll(field, -1, axis=2) - 4.0 * field)


def advance(adjoint, wet_mask, diffusive, mixing_m, coupling_m, forcing):
    masked = wet_mask * adjoint
    spread = laplace(diffusive * masked)
    mixing_term = jnp.einsum("dc,dyx->cyx", mixing_m, masked, precision=lax.Precision.HIGHEST)
    forced = jnp.einsum("cq,qyx->cyx", coupling_m, forcing, precision=lax.Precision.HIGHEST)
    return masked + spread + mixing_term + forced


def regrid_surface(surfaces, regrid, atmos_tile_index, ocean_block_index, atmos_block_index):
    per_tile_layout = surfaces.reshape(WINDOW_STEPS, COUPLING_FIELDS, N_GY, CY, N_GX, CX).transpose(2, 4, 0, 1, 3, 5)
    per_tile_layout = per_tile_layout.reshape(SECTION_TILES, WINDOW_STEPS, COUPLING_FIELDS, TILE_BLOCKS, BLOCK_GRID_CELLS)
    sources = ocean_block_index.reshape(SECTION_TILES, REGRID_ENTRIES).astype(jnp.int32)
    picked = jax.vmap(lambda tile_data, index_row: jnp.take(tile_data, index_row, axis=2))(per_tile_layout, sources)
    partials = jnp.einsum("tkqbc,tcd->tbkqd", picked, regrid, precision=lax.Precision.HIGHEST)
    destination_value = (atmos_tile_index.reshape(-1) * TILE_BLOCKS + atmos_block_index).astype(jnp.int32)
    accumulated_sum = jax.ops.segment_sum(partials.reshape(SECTION_TILES * REGRID_ENTRIES, WINDOW_STEPS, COUPLING_FIELDS, BLOCK_GRID_CELLS), destination_value,
                                 num_segments=SECTION_TILES * TILE_BLOCKS)
    accumulated_sum = accumulated_sum.reshape(N_GY, N_GX, TILE_BLOCKS, WINDOW_STEPS, COUPLING_FIELDS, BLOCK_GRID_CELLS).transpose(0, 1, 3, 4, 2, 5)
    accumulated_sum = accumulated_sum.reshape(N_GY, N_GX, WINDOW_STEPS, COUPLING_FIELDS, CY, CX).transpose(2, 3, 0, 4, 1, 5)
    return accumulated_sum.reshape(WINDOW_STEPS, COUPLING_FIELDS, NY, NX)


def reference(adjoint_init, diffusivity, mixing, coupling, history, extract, land_mask,
              regrid, atmos_tile_index, ocean_block_index, atmos_block_index):
    wet_mask = land_mask.astype(jnp.float32)
    ocean = adjoint_init[0]
    surfaces = [None] * WINDOW_STEPS
    for time_step in range(WINDOW_STEPS - 1, -1, -1):
        forcing = jnp.concatenate([history[0, time_step], history[1, time_step]], axis=0)
        ocean = advance(ocean, wet_mask, diffusivity[0], mixing[0], coupling[0], forcing)
        surfaces[time_step] = jnp.einsum("qc,cyx->qyx", extract, wet_mask * ocean,
                                         precision=lax.Precision.HIGHEST)
    received = regrid_surface(jnp.stack(surfaces), regrid, atmos_tile_index, ocean_block_index, atmos_block_index)
    atmos = adjoint_init[1]
    for time_step in range(WINDOW_STEPS - 1, -1, -1):
        forcing = jnp.concatenate([history[1, time_step], received[time_step]], axis=0)
        atmos = advance(atmos, 1.0, diffusivity[1], mixing[1], coupling[1], forcing)
    return jnp.stack([ocean, atmos])
```

```python
import math

import jax
import jax.numpy as jnp
from jax import lax
from jax.experimental import pallas as pl
from jax.experimental.pallas import tpu as pltpu
from jax.sharding import PartitionSpec as P

LANES = 128
SUB = 8
F32 = jnp.float32
BF16 = jnp.bfloat16


def full_dot(a, b, dims=(((1,), (0,)), ((), ()))):
    return lax.dot_general(a, b, dims, precision=lax.Precision.HIGHEST, preferred_element_type=F32)


def halves(x):
    high = x.astype(BF16)
    return high, (x - high.astype(F32)).astype(BF16)


def bf_dot(a, b, dims=(((1,), (0,)), ((), ()))):
    return lax.dot_general(a, b, dims, preferred_element_type=F32)


def dot3(a, b):
    (ah, al), (bh, bl) = a, b
    return bf_dot(ah, bh) + (bf_dot(ah, bl) + bf_dot(al, bh))


def grown(matrix):
    rows, cols = matrix.shape
    up = lax.broadcasted_iota(jnp.int32, (rows * SUB, rows), 0) // SUB
    up = (up == lax.broadcasted_iota(jnp.int32, (rows * SUB, rows), 1)).astype(F32)
    out = lax.broadcasted_iota(jnp.int32, (cols, cols * SUB), 1) // SUB
    out = (out == lax.broadcasted_iota(jnp.int32, (cols, cols * SUB), 0)).astype(F32)
    spread = full_dot(full_dot(up, matrix), out)
    i = lax.broadcasted_iota(jnp.int32, spread.shape, 0) % SUB
    j = lax.broadcasted_iota(jnp.int32, spread.shape, 1) % SUB
    return jnp.where(i == j, spread, 0.0)


def lane_ids(rows):
    return lax.broadcasted_iota(jnp.int32, (rows, LANES), 1)


def pack_columns(read, count, rows, tx, hw):
    per = LANES // hw
    ids = lane_ids(rows) // hw
    east, west = [], []
    last = tx // LANES - 1
    for block in range(-(-count // per)):
        e = jnp.zeros((rows, LANES), F32)
        w = jnp.zeros((rows, LANES), F32)
        for place in range(min(per, count - block * per)):
            f = block * per + place
            e_in, w_in = read(f, last), read(f, 0)
            e_shift, w_shift = (place * hw + hw) % LANES, place * hw
            e_in = pltpu.roll(e_in, e_shift, 1) if e_shift else e_in
            w_in = pltpu.roll(w_in, w_shift, 1) if w_shift else w_in
            e = jnp.where(ids == place, e_in, e)
            w = jnp.where(ids == place, w_in, w)
        east.append(e)
        west.append(w)
    return east, west


def side_block(from_west, from_east, f, hw):
    place = f % (LANES // hw)
    ids = lane_ids(from_west.shape[0])
    e_shift, w_shift = (-place * hw) % LANES, (-hw - place * hw) % LANES
    e = pltpu.roll(from_east, e_shift, 1) if e_shift else from_east
    w = pltpu.roll(from_west, w_shift, 1) if w_shift else from_west
    return jnp.where(ids < hw, e, jnp.where(ids >= LANES - hw, w, 0.0))


def pair_rows(a, b, first):
    low = lax.broadcasted_iota(jnp.int32, a.shape, 0) < SUB // 2
    turned = pltpu.roll(b, SUB // 2, 0)
    return jnp.where(low, a, turned) if first else jnp.where(low, turned, a)


def edge_tile(from_north, from_south, odd):
    if odd:
        from_north = pltpu.roll(from_north, SUB // 2, 0)
        from_south = pltpu.roll(from_south, SUB // 2, 0)
    low = lax.broadcasted_iota(jnp.int32, from_north.shape, 0) < SUB // 2
    return jnp.where(low, from_south, from_north)


def send_rows(read, count, ty, north_ref, south_ref):
    for pair in range(-(-count // 2)):
        a, b = 2 * pair, min(2 * pair + 1, count - 1)
        last = ty // SUB - 1
        north_ref[pair] = pair_rows(read(a, 0), read(b, 0), True)
        south_ref[pair] = pair_rows(read(a, last), read(b, last), False)


def ring_lap(p):
    rows, cols = p.shape
    around = pltpu.roll(p, 1, 0) + pltpu.roll(p, rows - 1, 0)
    around = around + pltpu.roll(p, 1, 1) + pltpu.roll(p, cols - 1, 1)
    return around - 4.0 * p


def with_ring(main, packed_west, packed_east, f, north_ref, south_ref, hw):
    bottom = edge_tile(north_ref[f // 2], south_ref[f // 2], f % 2)
    side = side_block(packed_west, packed_east, f, hw)
    return jnp.concatenate([jnp.concatenate([main, bottom], axis=0), side], axis=1)


def sides_with_rows(west_ref, east_ref, north_ref, south_ref, first, blocks, tx):
    west, east = [], []
    per = tx // LANES
    for block in range(blocks):
        lanes = pl.ds((block % per) * LANES, LANES)
        out = []
        for which, ref in enumerate((west_ref, east_ref)):
            f, at = divmod(which * blocks + block, per)
            f = first + f
            cols = pl.ds(at * LANES, LANES)
            tile = edge_tile(north_ref[f // 2, :, cols], south_ref[f // 2, :, cols], f % 2)
            out.append(jnp.concatenate([ref[:, pl.ds(block * LANES, LANES)], tile], axis=0))
        west.append(out[0])
        east.append(out[1])
    return west, east


def packed_reader(west_ref, east_ref, blocks, tx):
    per = tx // LANES

    def read(f, row_tile):
        pieces = []
        for at in range(per):
            which, block = divmod(f * per + at, blocks)
            rows = pl.ds(row_tile * SUB, SUB)
            if which < 2:
                pieces.append((west_ref, east_ref)[which][rows, pl.ds(block * LANES, LANES)])
            else:
                pieces.append(jnp.zeros((SUB, LANES), F32))
        return jnp.concatenate(pieces, axis=1)

    return read, -(-2 * blocks // per)


def call(kernel, outs, *args, smem=(), scratch=(), flops=0):
    space = lambda i: pltpu.SMEM if i in smem else pltpu.VMEM
    nbytes = sum(math.prod(a.shape) * 4 for a in (*args, *outs))
    return pl.pallas_call(
        kernel,
        out_shape=outs,
        in_specs=[pl.BlockSpec(memory_space=space(i)) for i in range(len(args))],
        out_specs=[pl.BlockSpec(memory_space=pltpu.VMEM) for _ in outs],
        scratch_shapes=scratch,
        compiler_params=pltpu.CompilerParams(vmem_limit_bytes=48 * 2**20),
        cost_estimate=pl.CostEstimate(flops=flops, bytes_accessed=nbytes, transcendentals=0),
    )(*args)


def tile_of(ref, g, l):
    block = ref[:, g * SUB : (g + 1) * SUB, l * LANES : (l + 1) * LANES]
    return block.reshape(-1, LANES)


def project_kernel(adj_ref, mask_ref, mix_ref, ext_ref, coup_ref, hist_ref, diff_ref, keep_ref, send_ref):
    _, nc, ty, tx = adj_ref.shape
    _, steps, fields = hist_ref.shape[:3]
    hf = fields // 2
    mix = mix_ref[0]
    rows = ext_ref[...]
    lows, highs = [], []
    for m in range(steps + 1):
        big = grown(rows)
        lows.append(big[: hf * SUB])
        highs.append(big[hf * SUB :])
        if m < steps:
            force = grown(full_dot(rows, coup_ref[0]))
            height, width = hf * SUB, force.shape[1]
            for ref, at in ((keep_ref, 0), (send_ref, height)):
                per = ty // height
                r0, c0 = (m % per) * height, (m // per) * LANES
                ref[(steps + 1) * hf, r0 : r0 + height, c0 : c0 + width] = force[at : at + height]
            rows = rows + full_dot(rows, mix, (((1,), (1,)), ((), ())))
    big = halves(jnp.concatenate(lows + highs, axis=0))
    count = (steps + 1) * hf
    for g in range(ty // SUB):
        for l in range(tx // LANES):
            rs, cs = slice(g * SUB, (g + 1) * SUB), slice(l * LANES, (l + 1) * LANES)
            wet = mask_ref[rs, cs].astype(F32)
            u = (adj_ref[0, :, rs, cs] * wet[None]).reshape(nc * SUB, LANES)
            t = dot3(big, halves(u)).reshape(2 * count, SUB, LANES)
            keep_ref[:count, rs, cs] = t[:count]
            send_ref[:count, rs, cs] = t[count:]
    send_ref[count + 1] = diff_ref[0]
    for k in range(steps):
        for q in range(fields):
            send_ref[count + 2 + k * fields + q] = hist_ref[0, k, q]


def field_places(steps, hf):
    with_halo, without = [], []
    for m in range(steps + 1):
        for q in range(hf):
            (with_halo if m < steps else without).append(("t", m, q))
    for n in range(steps):
        for m in range(steps - n):
            for q in range(hf):
                (with_halo if n + m < steps - 1 else without).append(("g", n, m, q))
    with_halo += ["d", "w"]
    return {key: i for i, key in enumerate(with_halo + without)}, len(with_halo)


def force_kernel(
    places, halo_count, flag_ref, keep_ref, got_ref, hist_ref, diff_ref, mask_ref, main_ref, east_ref, west_ref
):
    _, steps, fields, ty, tx = hist_ref.shape
    hf, hw = fields // 2, steps
    count = (steps + 1) * hf
    ocean = flag_ref[0] == 0
    pick = lambda a, b: jnp.where(ocean, a, b)
    for m in range(steps + 1):
        for q in range(hf):
            main_ref[places["t", m, q]] = pick(keep_ref[m * hf + q], got_ref[m * hf + q])
    main_ref[places["d"]] = pick(diff_ref[0], got_ref[count + 1])
    main_ref[places["w"]] = mask_ref[...].astype(F32)
    height, width = hf * SUB, 2 * fields * SUB
    per = ty // height
    big = []
    for m in range(steps):
        r0, c0 = (m % per) * height, (m // per) * LANES
        at = (count, slice(r0, r0 + height), slice(c0, c0 + width))
        big.append(pick(keep_ref[at], got_ref[at]))
    big = halves(jnp.concatenate(big, axis=0))
    for g in range(ty // SUB):
        for l in range(tx // LANES):
            rs, cs = slice(g * SUB, (g + 1) * SUB), slice(l * LANES, (l + 1) * LANES)
            for n in range(steps):
                k = steps - 1 - n
                own = hist_ref[0, k, :, rs, cs]
                far = got_ref[count + 2 + k * fields : count + 2 + (k + 1) * fields, rs, cs]
                h = jnp.concatenate([pick(own, far), pick(far, own)], axis=0).reshape(-1, LANES)
                top = (steps - n) * height
                out = dot3((big[0][:top], big[1][:top]), halves(h))
                for m in range(steps - n):
                    for q in range(hf):
                        at = (m * hf + q) * SUB
                        main_ref[places["g", n, m, q], rs, cs] = out[at : at + SUB]
    read = lambda f, l: main_ref[f, :, l * LANES : (l + 1) * LANES]
    east, west = pack_columns(read, halo_count, ty, tx, hw)
    for block, (e, w) in enumerate(zip(east, west)):
        east_ref[:, block * LANES : (block + 1) * LANES] = e
        west_ref[:, block * LANES : (block + 1) * LANES] = w


def rows_kernel(halo_count, blocks, main_ref, west_ref, east_ref, north_ref, south_ref):
    _, ty, tx = main_ref.shape
    packed, more = packed_reader(west_ref, east_ref, blocks, tx)

    def read(f, t):
        return main_ref[f, t * SUB : (t + 1) * SUB, :] if f < halo_count else packed(f - halo_count, t)

    send_rows(read, halo_count + more, ty, north_ref, south_ref)


def index_kernel(cap, slots, nb, pos_ref, dest_ref, src_ref, dst_ref, sel_ref, acc_ref):
    tiles, entries = dest_ref.shape
    tile = pos_ref[0]
    count = tiles * cap
    per_row = slots // nb
    place = lambda b: (b % nb) * per_row + b // nb
    row = lax.broadcasted_iota(jnp.int32, (entries, entries), 0)
    col = lax.broadcasted_iota(jnp.int32, (entries, entries), 1)
    dest = dest_ref[pl.ds(tile, 1), :]
    across = jnp.broadcast_to(dest.astype(F32), (entries, entries))
    same = (across == across.T) & (row < col)
    rank = jnp.sum(same.astype(F32), axis=0, keepdims=True).astype(jnp.int32)
    slot = dest * cap + rank
    last = (((1,), (1,)), ((), ()))

    def onehot(size, values):
        ids = lax.broadcasted_iota(jnp.int32, (size, entries), 0)
        return (ids == values).astype(F32).astype(BF16)

    sel_ref[...] = bf_dot(onehot(count, slot), onehot(slots, place(src_ref[pl.ds(tile, 1), :])), last)
    acc_ref[...] = jnp.zeros_like(acc_ref)
    before = (row < col).astype(F32).astype(BF16)

    def source(i, carry):
        mine = dest_ref[pl.ds(i, 1), :] == tile
        mine_f = jnp.broadcast_to(mine.astype(F32), (SUB, entries)).astype(BF16)
        ranks = bf_dot(mine_f, before)[:1].astype(jnp.int32)
        spot = jnp.where(mine, i * cap + ranks, -1)
        acc_ref[...] += bf_dot(onehot(slots, place(dst_ref[pl.ds(i, 1), :])), onehot(count, spot), last)
        return carry

    lax.fori_loop(0, tiles, source, 0)


def surface_kernel(
    places, halo_count, steps, hf, main_ref, west_ref, east_ref, north_ref, south_ref, regrid_ref, sel_ref, out_ref
):
    _, ty, tx = main_ref.shape
    hw = steps
    per = LANES // hw
    blocks = -(-halo_count // per)
    wests, easts = sides_with_rows(west_ref, east_ref, north_ref, south_ref, halo_count, blocks, tx)

    def ext(key):
        f = places[key]
        if f < halo_count:
            return with_ring(main_ref[f], wests[f // per], easts[f // per], f, north_ref, south_ref, hw)
        main = jnp.concatenate([main_ref[f], jnp.zeros((SUB, tx), F32)], axis=0)
        return jnp.concatenate([main, jnp.zeros((ty + SUB, LANES), F32)], axis=1)

    diff, wet = ext("d"), ext("w")
    weights = halves(regrid_ref[0])
    sel = sel_ref[...].astype(BF16)
    surfaces = {}
    for q in range(hf):
        t = [ext(("t", m, q)) for m in range(steps + 1)]
        for n in range(steps):
            t = [wet * (t[m + 1] + ring_lap(diff * t[m]) + ext(("g", n, m, q))) for m in range(steps - n)]
            surfaces[n, q] = t[0]
    for n in range(steps):
        for q in range(hf):
            s = surfaces[n, q]
            s = jnp.concatenate([s[:ty, l * LANES : (l + 1) * LANES] for l in range(tx // LANES)], axis=0)
            s = halves(dot3(halves(s), weights))
            at = (n * hf + q) * LANES
            out_ref[:, at : at + LANES] = bf_dot(sel, s[0]) + bf_dot(sel, s[1])


def gather_kernel(acc_ref, in_ref, out_ref):
    count, ty, tx = out_ref.shape
    acc = acc_ref[...].astype(BF16)
    for i in range(count):
        high, low = halves(in_ref[:, i * LANES : (i + 1) * LANES])
        total = bf_dot(acc, high) + bf_dot(acc, low)
        for l in range(tx // LANES):
            out_ref[i, :, l * LANES : (l + 1) * LANES] = total[l * ty : (l + 1) * ty]


def state_reader(adj_ref, hist_ref, far_ref, far_at, diff_ref, wet):
    _, steps, fields = hist_ref.shape[:3]
    nc = adj_ref.shape[1]
    forced = (steps - 1) * fields
    total = nc + 2 * forced + 2

    def read(f, rows, cols):
        if f < nc:
            return adj_ref[0, f, rows, cols]
        f -= nc
        if f < 2 * forced:
            part, f = divmod(f, forced)
            k, q = divmod(f, fields)
            if part == 0:
                return hist_ref[0, k + 1, q, rows, cols]
            return far_ref[far_at + (k + 1) * fields + q, rows, cols]
        if f == 2 * forced:
            return diff_ref[0, rows, cols]
        return wet(rows, cols)

    return read, total


def own_wet(flag_ref, mask_ref):
    ocean = flag_ref[0] == 0
    return lambda rows, cols: jnp.where(ocean, mask_ref[rows, cols].astype(F32), 1.0)


def state_columns_kernel(far_at, flag_ref, adj_ref, hist_ref, far_ref, diff_ref, mask_ref, east_ref, west_ref):
    ty, tx = mask_ref.shape
    hw = hist_ref.shape[1]
    read, total = state_reader(adj_ref, hist_ref, far_ref, far_at, diff_ref, own_wet(flag_ref, mask_ref))
    at = lambda f, l: read(f, slice(0, ty), slice(l * LANES, (l + 1) * LANES))
    east, west = pack_columns(at, total, ty, tx, hw)
    for block, (e, w) in enumerate(zip(east, west)):
        east_ref[:, block * LANES : (block + 1) * LANES] = e
        west_ref[:, block * LANES : (block + 1) * LANES] = w


def state_rows_kernel(
    far_at, blocks, flag_ref, adj_ref, hist_ref, far_ref, diff_ref, mask_ref, west_ref, east_ref, north_ref, south_ref
):
    ty, tx = mask_ref.shape
    read, total = state_reader(adj_ref, hist_ref, far_ref, far_at, diff_ref, own_wet(flag_ref, mask_ref))
    packed, more = packed_reader(west_ref, east_ref, blocks, tx)

    def at(f, t):
        rows = slice(t * SUB, (t + 1) * SUB)
        return read(f, rows, slice(0, tx)) if f < total else packed(f - total, t)

    send_rows(at, total + more, ty, north_ref, south_ref)


def state_kernel(
    far_at,
    blocks,
    flag_ref,
    adj_ref,
    hist_ref,
    far_ref,
    diff_ref,
    mask_ref,
    west_ref,
    east_ref,
    north_ref,
    south_ref,
    mix_ref,
    coup_ref,
    out_ref,
    ring_ref,
    late_ref,
    state,
    force,
    spread,
):
    ty, tx = mask_ref.shape
    nc = adj_ref.shape[1]
    _, steps, fields = hist_ref.shape[:3]
    hw = steps
    per = LANES // hw
    ocean = flag_ref[0] == 0
    read, total = state_reader(adj_ref, hist_ref, far_ref, far_at, diff_ref, own_wet(flag_ref, mask_ref))
    wests, easts = sides_with_rows(west_ref, east_ref, north_ref, south_ref, total, blocks, tx)

    def ext(f):
        main = read(f, slice(0, ty), slice(0, tx))
        return with_ring(main, wests[f // per], easts[f // per], f, north_ref, south_ref, hw)

    for c in range(nc):
        state[c] = ext(c)
    forced = (steps - 1) * fields
    for k in range(1, steps):
        for q in range(fields):
            force[k, q] = ext(nc + (k - 1) * fields + q)
            force[k, fields + q] = ext(nc + forced + (k - 1) * fields + q)
    for q in range(fields):
        force[0, q, :ty, :tx] = hist_ref[0, 0, q]
        force[0, fields + q, :ty, :tx] = far_ref[far_at + q]
    diff, wet = ext(nc + 2 * forced), ext(nc + 2 * forced + 1)
    ring_ref[...] = diff
    ident = lax.broadcasted_iota(jnp.int32, (nc, nc), 0) == lax.broadcasted_iota(jnp.int32, (nc, nc), 1)
    step_m = mix_ref[0].T + ident.astype(F32)
    coup = coup_ref[0]
    late = coup[:, fields:]
    powers = []
    for i in range(steps):
        powers.append(late)
        late = full_dot(step_m, late)
    columns = []
    for k in range(steps - 1, -1, -1):
        for j in range(k + 1):
            columns.append(math.comb(k, j) * powers[k - j])
    at = 0
    for column in columns:
        late_ref[:, at : at + fields * SUB] = grown(column)
        at += fields * SUB
    first = lax.broadcasted_iota(jnp.int32, coup.shape, 1) < fields
    coup = jnp.where(jnp.logical_or(first, ocean), coup, 0.0)
    mix8, coup8 = halves(grown(step_m)), halves(grown(coup))

    for n in range(steps):
        k = steps - 1 - n
        small = n == steps - 1

        def one(c, carry):
            u = wet * state[c]
            state[c] = u
            spread[c] = ring_lap(diff * u)
            return carry

        lax.fori_loop(0, nc, one, 0)
        for g in range(ty // SUB + (not small)):
            for l in range(tx // LANES + (not small)):
                rs, cs = slice(g * SUB, (g + 1) * SUB), slice(l * LANES, (l + 1) * LANES)
                u = state[:, rs, cs].reshape(nc * SUB, LANES)
                h = force[k, :, rs, cs].reshape(2 * fields * SUB, LANES)
                new = dot3(mix8, halves(u)) + dot3(coup8, halves(h))
                new = new.reshape(nc, SUB, LANES) + spread[:, rs, cs]
                if small:
                    out_ref[:, rs, cs] = new
                else:
                    state[:, rs, cs] = new


def late_fields(steps, fields):
    return [(n, q) for n in range(steps - 1) for q in range(fields)]


def late_main(steps, hf, own_ref, far_ref):
    def read(n, q):
        return far_ref[n * hf + q] if q < hf else own_ref[n * hf + q - hf]

    return read


def late_columns_kernel(steps, own_ref, far_ref, east_ref, west_ref):
    count, ty, tx = own_ref.shape
    hf = count // steps
    todo = late_fields(steps, 2 * hf)

    def read(f, l):
        n, q = todo[f]
        ref, i = (far_ref, n * hf + q) if q < hf else (own_ref, n * hf + q - hf)
        return ref[i, :, l * LANES : (l + 1) * LANES]

    east, west = pack_columns(read, len(todo), ty, tx, steps)
    for block, (e, w) in enumerate(zip(east, west)):
        east_ref[:, block * LANES : (block + 1) * LANES] = e
        west_ref[:, block * LANES : (block + 1) * LANES] = w


def late_rows_kernel(steps, blocks, own_ref, far_ref, west_ref, east_ref, north_ref, south_ref):
    count, ty, tx = own_ref.shape
    hf = count // steps
    todo = late_fields(steps, 2 * hf)
    packed, more = packed_reader(west_ref, east_ref, blocks, tx)

    def read(f, t):
        if f >= len(todo):
            return packed(f - len(todo), t)
        n, q = todo[f]
        ref, i = (far_ref, n * hf + q) if q < hf else (own_ref, n * hf + q - hf)
        return ref[i, t * SUB : (t + 1) * SUB, :]

    send_rows(read, len(todo) + more, ty, north_ref, south_ref)


def late_kernel(
    steps,
    blocks,
    flag_ref,
    base_ref,
    ring_ref,
    late_ref,
    own_ref,
    far_ref,
    west_ref,
    east_ref,
    north_ref,
    south_ref,
    out_ref,
    stack,
):
    count, ty, tx = own_ref.shape
    hf = count // steps
    fields = 2 * hf
    nc = base_ref.shape[0]
    per = LANES // steps
    todo = late_fields(steps, fields)
    read = late_main(steps, hf, own_ref, far_ref)

    @pl.when(flag_ref[0] == 0)
    def _():
        out_ref[0] = base_ref[...]

    @pl.when(flag_ref[0] != 0)
    def _():
        diff = ring_ref[...]
        wests, easts = sides_with_rows(west_ref, east_ref, north_ref, south_ref, len(todo), blocks, tx)
        at = 0
        for n in range(steps):
            k = steps - 1 - n
            for q in range(fields):
                r = read(n, q)
                if k:
                    f = todo.index((n, q))
                    r = with_ring(r, wests[f // per], easts[f // per], f, north_ref, south_ref, steps)
                for j in range(k + 1):
                    stack[at + j * fields + q] = r[:ty, :tx]
                    if j < k:
                        r = ring_lap(diff * r)
            at += (k + 1) * fields
        big = halves(late_ref[...])
        for g in range(ty // SUB):
            for l in range(tx // LANES):
                rs, cs = slice(g * SUB, (g + 1) * SUB), slice(l * LANES, (l + 1) * LANES)
                more = dot3(big, halves(stack[:, rs, cs].reshape(-1, LANES)))
                out_ref[0, :, rs, cs] = base_ref[:, rs, cs] + more.reshape(nc, SUB, LANES)


def shifted(x, axis, by, wrap, sect=None):
    size = lax.axis_size(axis)
    pairs = [(i, (i + by) % size) for i in range(size) if wrap or 0 <= i + by < size]
    if sect is None:
        return lax.ppermute(x, axis, pairs)
    base = sect * size
    return lax.ppermute(x, ("sect", axis), [(base + i, base + j) for i, j in pairs])


def struct(*shape):
    return jax.ShapeDtypeStruct(shape, F32)


def partial(kernel, *args):
    def run(*refs):
        kernel(*args, *refs)

    run.__name__ = kernel.__name__
    return run


def body(
    adjoint_init,
    diffusivity,
    mixing,
    coupling,
    history,
    extract,
    land_mask,
    regrid,
    atmos_tile_index,
    ocean_block_index,
    atmos_block_index,
):
    _, steps, fields, ty, tx = history.shape
    nc = adjoint_init.shape[1]
    hf, hw = fields // 2, steps
    per = LANES // hw
    sect = lax.axis_index("sect").astype(jnp.int32)
    tile = (lax.axis_index("gy") * lax.axis_size("gx") + lax.axis_index("gx")).astype(jnp.int32)
    flag = sect.reshape(1)
    tiles = lax.axis_size("gy") * lax.axis_size("gx")
    entries = ocean_block_index.shape[0] // tiles
    cap = 2 * entries // tiles
    cells = regrid.shape[1]
    slots = ty * tx // cells
    nb = tx // cells

    def exchange(x_after, x_before, axis, wrap, only=None):
        return shifted(x_after, axis, 1, wrap, only), shifted(x_before, axis, -1, wrap, only)

    count = (steps + 1) * hf
    keep, send = call(
        project_kernel,
        [struct(count + 1, ty, tx), struct(count + 2 + steps * fields, ty, tx)],
        adjoint_init, land_mask, mixing, extract, coupling, history, diffusivity,
    )
    got = lax.ppermute(send, "sect", [(0, 1), (1, 0)])
    places, halo_count = field_places(steps, hf)
    blocks = -(-halo_count // per)
    main, east, west = call(
        partial(force_kernel, places, halo_count),
        [struct(len(places), ty, tx), struct(ty, blocks * LANES), struct(ty, blocks * LANES)],
        flag, keep, got, history, diffusivity, land_mask,
        smem=(0,),
    )
    from_west, from_east = exchange(east, west, "gx", True)
    pairs = -(-(halo_count + -(-2 * blocks * LANES // tx)) // 2)
    north, south = call(
        partial(rows_kernel, halo_count, blocks),
        [struct(pairs, SUB, tx)] * 2,
        main, from_west, from_east,
    )
    from_north, from_south = exchange(south, north, "gy", False)
    sel, acc = call(
        partial(index_kernel, cap, slots, nb),
        [struct(tiles * cap, slots), struct(slots, tiles * cap)],
        tile.reshape(1),
        atmos_tile_index.reshape(tiles, entries),
        ocean_block_index.reshape(tiles, entries),
        atmos_block_index.reshape(tiles, entries),
        smem=(0,),
    )
    [packed] = call(
        partial(surface_kernel, places, halo_count, steps, hf),
        [struct(tiles * cap, steps * hf * LANES)],
        main, from_west, from_east, from_north, from_south, regrid, sel,
    )
    arrived = lax.all_to_all(
        packed.reshape(tiles, cap, -1), ("gy", "gx"), split_axis=0, concat_axis=0, tiled=True
    ).reshape(tiles * cap, -1)

    far_at = count + 2
    total = nc + 2 * (steps - 1) * fields + 2
    blocks = -(-total // per)
    east, west = call(
        partial(state_columns_kernel, far_at),
        [struct(ty, blocks * LANES)] * 2,
        flag, adjoint_init, history, got, diffusivity, land_mask,
        smem=(0,),
    )
    from_west, from_east = exchange(east, west, "gx", True)
    pairs = -(-(total + -(-2 * blocks * LANES // tx)) // 2)
    north, south = call(
        partial(state_rows_kernel, far_at, blocks),
        [struct(pairs, SUB, tx)] * 2,
        flag, adjoint_init, history, got, diffusivity, land_mask, from_west, from_east,
        smem=(0,),
    )
    from_north, from_south = exchange(south, north, "gy", False)
    terms = fields * steps * (steps + 1) // 2
    ext = (ty + SUB, tx + LANES)
    base, ring, late = call(
        partial(state_kernel, far_at, blocks),
        [struct(nc, ty, tx), struct(*ext), struct(nc * SUB, terms * SUB)],
        flag, adjoint_init, history, got, diffusivity, land_mask,
        from_west, from_east, from_north, from_south, mixing, coupling,
        smem=(0,),
        scratch=[
            pltpu.VMEM((nc, *ext), F32),
            pltpu.VMEM((steps, 2 * fields, *ext), F32),
            pltpu.VMEM((nc, *ext), F32),
        ],
    )

    [own] = call(gather_kernel, [struct(steps * hf, ty, tx)], acc, arrived)
    far = lax.ppermute(own, "sect", [(0, 1)])
    halo_count = (steps - 1) * fields
    blocks = -(-halo_count // per)
    east, west = call(partial(late_columns_kernel, steps), [struct(ty, blocks * LANES)] * 2, own, far)
    from_west, from_east = exchange(east, west, "gx", True, 1) if False else exchange(east, west, "gx", True)
    pairs = -(-(halo_count + -(-2 * blocks * LANES // tx)) // 2)
    north, south = call(
        partial(late_rows_kernel, steps, blocks), [struct(pairs, SUB, tx)] * 2, own, far, from_west, from_east
    )
    from_north, from_south = exchange(south, north, "gy", False)
    [out] = call(
        partial(late_kernel, steps, blocks),
        [struct(1, nc, ty, tx)],
        flag, base, ring, late, own, far, from_west, from_east, from_north, from_south,
        smem=(0,),
        scratch=[pltpu.VMEM((terms, ty, tx), F32)],
    )
    return out


def solution(mesh):
    placed = (
        P("sect", None, "gy", "gx"),
        P("sect", "gy", "gx"),
        P("sect", None, None),
        P("sect", None, None),
        P("sect", None, None, "gy", "gx"),
        P(),
        P("gy", "gx"),
        P(("gy", "gx"), None, None),
        P(),
        P(),
        P(),
    )
    return jax.shard_map(
        body, mesh=mesh, in_specs=placed, out_specs=P("sect", None, "gy", "gx"), check_vma=False
    )
```

```python
import math

import jax
import jax.numpy as jnp
from jax import lax
from jax.experimental import pallas as pl
from jax.experimental.pallas import tpu as pltpu
from jax.sharding import PartitionSpec as P

LANES = 128
SUB = 8
F32 = jnp.float32
BF16 = jnp.bfloat16


LAST = (((1,), (1,)), ((), ()))


def full_dot(a, b, dims=(((1,), (0,)), ((), ()))):
    return lax.dot_general(a, b, dims, precision=lax.Precision.HIGHEST, preferred_element_type=F32)


def halves(x):
    high = x.astype(BF16)
    return high, (x - high.astype(F32)).astype(BF16)


def bf_dot(a, b, dims=(((1,), (0,)), ((), ()))):
    return lax.dot_general(a, b, dims, preferred_element_type=F32)


def dot3(a, b):
    (ah, al), (bh, bl) = a, b
    return bf_dot(ah, bh) + (bf_dot(ah, bl) + bf_dot(al, bh))


def grown(matrix):
    rows, cols = matrix.shape
    up = lax.broadcasted_iota(jnp.int32, (rows * SUB, rows), 0) // SUB
    up = (up == lax.broadcasted_iota(jnp.int32, (rows * SUB, rows), 1)).astype(F32)
    out = lax.broadcasted_iota(jnp.int32, (cols, cols * SUB), 1) // SUB
    out = (out == lax.broadcasted_iota(jnp.int32, (cols, cols * SUB), 0)).astype(F32)
    spread = full_dot(full_dot(up, matrix), out)
    i = lax.broadcasted_iota(jnp.int32, spread.shape, 0) % SUB
    j = lax.broadcasted_iota(jnp.int32, spread.shape, 1) % SUB
    return jnp.where(i == j, spread, 0.0)


def lane_ids(rows):
    return lax.broadcasted_iota(jnp.int32, (rows, LANES), 1)


def pack_columns(read, count, rows, tx, hw):
    per = LANES // hw
    ids = lane_ids(rows) // hw
    east, west = [], []
    last = tx // LANES - 1
    for block in range(-(-count // per)):
        e = jnp.zeros((rows, LANES), F32)
        w = jnp.zeros((rows, LANES), F32)
        for place in range(min(per, count - block * per)):
            f = block * per + place
            e_in, w_in = read(f, last), read(f, 0)
            e_shift, w_shift = (place * hw + hw) % LANES, place * hw
            e_in = pltpu.roll(e_in, e_shift, 1) if e_shift else e_in
            w_in = pltpu.roll(w_in, w_shift, 1) if w_shift else w_in
            e = jnp.where(ids == place, e_in, e)
            w = jnp.where(ids == place, w_in, w)
        east.append(e)
        west.append(w)
    return east, west


def side_block(from_west, from_east, f, hw):
    place = f % (LANES // hw)
    ids = lane_ids(from_west.shape[0])
    e_shift, w_shift = (-place * hw) % LANES, (-hw - place * hw) % LANES
    e = pltpu.roll(from_east, e_shift, 1) if e_shift else from_east
    w = pltpu.roll(from_west, w_shift, 1) if w_shift else from_west
    return jnp.where(ids < hw, e, jnp.where(ids >= LANES - hw, w, 0.0))


def pair_rows(a, b, first):
    low = lax.broadcasted_iota(jnp.int32, a.shape, 0) < SUB // 2
    turned = pltpu.roll(b, SUB // 2, 0)
    return jnp.where(low, a, turned) if first else jnp.where(low, turned, a)


def edge_tile(from_north, from_south, odd):
    if odd:
        from_north = pltpu.roll(from_north, SUB // 2, 0)
        from_south = pltpu.roll(from_south, SUB // 2, 0)
    low = lax.broadcasted_iota(jnp.int32, from_north.shape, 0) < SUB // 2
    return jnp.where(low, from_south, from_north)


def send_rows(read, count, ty, north_ref, south_ref):
    for pair in range(-(-count // 2)):
        a, b = 2 * pair, min(2 * pair + 1, count - 1)
        last = ty // SUB - 1
        north_ref[pair] = pair_rows(read(a, 0), read(b, 0), True)
        south_ref[pair] = pair_rows(read(a, last), read(b, last), False)


def ring_lap(p):
    rows, cols = p.shape
    around = pltpu.roll(p, 1, 0) + pltpu.roll(p, rows - 1, 0)
    around = around + pltpu.roll(p, 1, 1) + pltpu.roll(p, cols - 1, 1)
    return around - 4.0 * p


def with_ring(main, packed_west, packed_east, f, north_ref, south_ref, hw):
    bottom = edge_tile(north_ref[f // 2], south_ref[f // 2], f % 2)
    side = side_block(packed_west, packed_east, f, hw)
    return jnp.concatenate([jnp.concatenate([main, bottom], axis=0), side], axis=1)


def sides_with_rows(west_ref, east_ref, north_ref, south_ref, first, start, blocks, tx):
    west, east = [], []
    per = tx // LANES
    for block in range(blocks):
        out = []
        for which, ref in enumerate((west_ref, east_ref)):
            f, at = divmod(which * blocks + block, per)
            f = first + f
            cols = pl.ds(at * LANES, LANES)
            tile = edge_tile(north_ref[f // 2, :, cols], south_ref[f // 2, :, cols], f % 2)
            out.append(jnp.concatenate([ref[:, pl.ds((start + block) * LANES, LANES)], tile], axis=0))
        west.append(out[0])
        east.append(out[1])
    return west, east


def packed_reader(west_ref, east_ref, start, blocks, tx):
    per = tx // LANES

    def read(f, row_tile):
        pieces = []
        for at in range(per):
            which, block = divmod(f * per + at, blocks)
            rows = pl.ds(row_tile * SUB, SUB)
            if which < 2:
                pieces.append((west_ref, east_ref)[which][rows, pl.ds((start + block) * LANES, LANES)])
            else:
                pieces.append(jnp.zeros((SUB, LANES), F32))
        return jnp.concatenate(pieces, axis=1)

    return read, -(-2 * blocks // per)


def call(kernel, outs, *args, smem=(), hbm=(), scratch=(), flops=0, vmem=48):
    space = lambda i: pltpu.SMEM if i in smem else pltpu.HBM if i in hbm else pltpu.VMEM
    nbytes = sum(math.prod(a.shape) * 4 for a in (*args, *outs))
    return pl.pallas_call(
        kernel,
        out_shape=outs,
        in_specs=[pl.BlockSpec(memory_space=space(i)) for i in range(len(args))],
        out_specs=[pl.BlockSpec(memory_space=pltpu.VMEM) for _ in outs],
        scratch_shapes=scratch,
        compiler_params=pltpu.CompilerParams(vmem_limit_bytes=vmem * 2**20),
        cost_estimate=pl.CostEstimate(flops=flops, bytes_accessed=nbytes, transcendentals=0),
    )(*args)


def stacked_rows(parts):
    high, low = halves(parts)
    return jnp.concatenate([high, high, low], axis=1)


def stacked_columns(parts):
    high, low = halves(parts)
    return jnp.concatenate([high, low, high], axis=0)


def project_kernel(
    adj_hbm, mask_hbm, diff_hbm, hist_hbm, mix_ref, ext_ref, coup_ref, keep_ref, send_ref, adj_ref, mask_ref, sems
):
    _, nc, ty, tx = adj_hbm.shape
    _, steps, fields = hist_hbm.shape[:3]
    hf = fields // 2
    count = (steps + 1) * hf
    copies = [
        pltpu.make_async_copy(mask_hbm, mask_ref, sems.at[0]),
        pltpu.make_async_copy(adj_hbm.at[0], adj_ref, sems.at[1]),
        pltpu.make_async_copy(diff_hbm.at[0], send_ref.at[count + 1], sems.at[2]),
    ]
    for k in range(steps):
        to = send_ref.at[pl.ds(count + 2 + k * fields, fields)]
        copies.append(pltpu.make_async_copy(hist_hbm.at[0, k], to, sems.at[3 + k]))
    for copy in copies:
        copy.start()
    mix = mix_ref[0]
    rows = ext_ref[...]
    lows, highs = [], []
    for m in range(steps + 1):
        big = grown(rows)
        lows.append(big[: hf * SUB])
        highs.append(big[hf * SUB :])
        if m < steps:
            force = grown(full_dot(rows, coup_ref[0], LAST))
            height, width = hf * SUB, force.shape[1]
            for ref, at in ((keep_ref, 0), (send_ref, height)):
                per = ty // height
                r0, c0 = (m % per) * height, (m // per) * LANES
                ref[count, r0 : r0 + height, c0 : c0 + width] = force[at : at + height]
            rows = rows + full_dot(rows, mix, LAST)
    big = halves(jnp.concatenate(lows + highs, axis=0))
    copies[0].wait()
    copies[1].wait()
    for g in range(ty // SUB):
        rs = slice(g * SUB, (g + 1) * SUB)
        wet = mask_ref[rs, :].astype(F32)
        u = (adj_ref[:, rs, :] * wet[None]).reshape(nc * SUB, tx)
        t = dot3(big, halves(u)).reshape(2 * count, SUB, tx)
        keep_ref[:count, rs, :] = t[:count]
        send_ref[:count, rs, :] = t[count:]
    for copy in copies[2:]:
        copy.wait()


def field_places(steps, hf):
    with_halo, without = [], []
    for m in range(steps + 1):
        for q in range(hf):
            (with_halo if m < steps else without).append(("t", m, q))
    for n in range(steps):
        for m in range(steps - n):
            for q in range(hf):
                (with_halo if n + m < steps - 1 else without).append(("g", n, m, q))
    with_halo += ["d", "w"]
    return {key: i for i, key in enumerate(with_halo + without)}, len(with_halo)


def force_kernel(
    places, halo_count, flag_ref, keep_ref, got_ref, adj_ref, hist_ref, diff_ref, mask_ref, main_ref, east_ref, west_ref
):
    _, steps, fields, ty, tx = hist_ref.shape
    hf, hw = fields // 2, steps
    count = (steps + 1) * hf
    ocean = flag_ref[0] == 0
    pick = lambda a, b: jnp.where(ocean, a, b)
    for m in range(steps + 1):
        for q in range(hf):
            main_ref[places["t", m, q]] = pick(keep_ref[m * hf + q], got_ref[m * hf + q])
    main_ref[places["d"]] = pick(diff_ref[0], got_ref[count + 1])
    main_ref[places["w"]] = mask_ref[...].astype(F32)
    height, width = hf * SUB, 2 * fields * SUB
    per = ty // height
    big = []
    for m in range(steps):
        r0, c0 = (m % per) * height, (m // per) * LANES
        at = (count, slice(r0, r0 + height), slice(c0, c0 + width))
        big.append(pick(keep_ref[at], got_ref[at]))
    big = stacked_rows(jnp.concatenate(big, axis=0))
    for g in range(ty // SUB):
        rs = slice(g * SUB, (g + 1) * SUB)
        for n in range(steps):
            k = steps - 1 - n
            own = hist_ref[0, k, :, rs, :]
            far = got_ref[count + 2 + k * fields : count + 2 + (k + 1) * fields, rs, :]
            h = jnp.concatenate([pick(own, far), pick(far, own)], axis=0).reshape(-1, tx)
            out = bf_dot(big[: (steps - n) * height], stacked_columns(h))
            for m in range(steps - n):
                for q in range(hf):
                    at = (m * hf + q) * SUB
                    main_ref[places["g", n, m, q], rs, :] = out[at : at + SUB]
    read = lambda f, l: main_ref[f, :, l * LANES : (l + 1) * LANES]
    east, west = pack_columns(read, halo_count, ty, tx, hw)
    state, total = state_reader(adj_ref, hist_ref, got_ref, count + 2, diff_ref, own_wet(flag_ref, mask_ref))
    read = lambda f, l: state(f, slice(0, ty), slice(l * LANES, (l + 1) * LANES))
    more = pack_columns(read, total, ty, tx, hw)
    for block, (e, w) in enumerate(zip(east + more[0], west + more[1])):
        east_ref[:, block * LANES : (block + 1) * LANES] = e
        west_ref[:, block * LANES : (block + 1) * LANES] = w


def rows_kernel(halo_count, blocks, main_ref, west_ref, east_ref, north_ref, south_ref):
    _, ty, tx = main_ref.shape
    packed, more = packed_reader(west_ref, east_ref, 0, blocks, tx)

    def read(f, t):
        return main_ref[f, t * SUB : (t + 1) * SUB, :] if f < halo_count else packed(f - halo_count, t)

    send_rows(read, halo_count + more, ty, north_ref, south_ref)


def block_place(slots, nb):
    return lambda b: (b % nb) * (slots // nb) + b // nb


def onehot(size, values):
    ids = lax.broadcasted_iota(jnp.int32, (size, values.shape[1]), 0)
    return (ids == values).astype(F32).astype(BF16)


def earlier(entries):
    row = lax.broadcasted_iota(jnp.int32, (entries, entries), 0)
    return row < lax.broadcasted_iota(jnp.int32, (entries, entries), 1)


def select_kernel(cap, slots, nb, pos_ref, dest_ref, src_ref, sel_ref):
    tiles, entries = dest_ref.shape
    tile = pos_ref[0]
    dest = dest_ref[pl.ds(tile, 1), :]
    across = jnp.broadcast_to(dest.astype(F32), (entries, entries))
    same = (across == across.T) & earlier(entries)
    rank = jnp.sum(same.astype(F32), axis=0, keepdims=True).astype(jnp.int32)
    source = block_place(slots, nb)(src_ref[pl.ds(tile, 1), :])
    sel_ref[...] = bf_dot(onehot(tiles * cap, dest * cap + rank), onehot(slots, source), LAST)


def arrival_kernel(cap, slots, nb, pos_ref, dest_ref, dst_ref, acc_ref):
    tiles, entries = dest_ref.shape
    tile = pos_ref[0]
    acc_ref[...] = jnp.zeros_like(acc_ref)
    before = earlier(entries).astype(F32).astype(BF16)

    def source(i, carry):
        mine = dest_ref[pl.ds(i, 1), :] == tile
        mine_f = jnp.broadcast_to(mine.astype(F32), (SUB, entries)).astype(BF16)
        ranks = bf_dot(mine_f, before)[:1].astype(jnp.int32)
        spot = jnp.where(mine, i * cap + ranks, -1)
        place = block_place(slots, nb)(dst_ref[pl.ds(i, 1), :])
        acc_ref[...] += bf_dot(onehot(slots, place), onehot(tiles * cap, spot), LAST)
        return carry

    lax.fori_loop(0, tiles, source, 0, unroll=4)


def surface_kernel(
    places, halo_count, steps, hf, main_ref, west_ref, east_ref, north_ref, south_ref, regrid_ref, sel_ref, out_ref
):
    _, ty, tx = main_ref.shape
    hw = steps
    per = LANES // hw
    blocks = -(-halo_count // per)
    wests, easts = sides_with_rows(west_ref, east_ref, north_ref, south_ref, halo_count, 0, blocks, tx)

    def ext(key):
        f = places[key]
        if f < halo_count:
            return with_ring(main_ref[f], wests[f // per], easts[f // per], f, north_ref, south_ref, hw)
        main = jnp.concatenate([main_ref[f], jnp.zeros((SUB, tx), F32)], axis=0)
        return jnp.concatenate([main, jnp.zeros((ty + SUB, LANES), F32)], axis=1)

    diff, wet = ext("d"), ext("w")
    weights = halves(regrid_ref[0])
    sel = sel_ref[...].astype(BF16)
    surfaces = {}
    for q in range(hf):
        t = [ext(("t", m, q)) for m in range(steps + 1)]
        for n in range(steps):
            t = [wet * (t[m + 1] + ring_lap(diff * t[m]) + ext(("g", n, m, q))) for m in range(steps - n)]
            surfaces[n, q] = t[0]
    for n in range(steps):
        for q in range(hf):
            s = surfaces[n, q]
            s = jnp.concatenate([s[:ty, l * LANES : (l + 1) * LANES] for l in range(tx // LANES)], axis=0)
            s = halves(dot3(halves(s), weights))
            at = (n * hf + q) * LANES
            out_ref[:, at : at + LANES] = bf_dot(sel, s[0]) + bf_dot(sel, s[1])


def gather_kernel(acc_ref, in_ref, out_ref):
    count, ty, tx = out_ref.shape
    acc = acc_ref[...].astype(BF16)
    for i in range(count):
        high, low = halves(in_ref[:, i * LANES : (i + 1) * LANES])
        total = bf_dot(acc, high) + bf_dot(acc, low)
        for l in range(tx // LANES):
            out_ref[i, :, l * LANES : (l + 1) * LANES] = total[l * ty : (l + 1) * ty]


def state_reader(adj_ref, hist_ref, far_ref, far_at, diff_ref, wet):
    _, steps, fields = hist_ref.shape[:3]
    nc = adj_ref.shape[1]
    forced = (steps - 1) * fields
    total = nc + 2 * forced + 2

    def read(f, rows, cols):
        if f < nc:
            return adj_ref[0, f, rows, cols]
        f -= nc
        if f < 2 * forced:
            part, f = divmod(f, forced)
            k, q = divmod(f, fields)
            if part == 0:
                return hist_ref[0, k + 1, q, rows, cols]
            return far_ref[far_at + (k + 1) * fields + q, rows, cols]
        if f == 2 * forced:
            return diff_ref[0, rows, cols]
        return wet(rows, cols)

    return read, total


def own_wet(flag_ref, mask_ref):
    ocean = flag_ref[0] == 0
    return lambda rows, cols: jnp.where(ocean, mask_ref[rows, cols].astype(F32), 1.0)


def state_rows_kernel(
    far_at, start, blocks, flag_ref, adj_ref, hist_ref, far_ref, diff_ref, mask_ref, west_ref, east_ref, north_ref, south_ref
):
    ty, tx = mask_ref.shape
    read, total = state_reader(adj_ref, hist_ref, far_ref, far_at, diff_ref, own_wet(flag_ref, mask_ref))
    packed, more = packed_reader(west_ref, east_ref, start, blocks, tx)

    def at(f, t):
        rows = slice(t * SUB, (t + 1) * SUB)
        return read(f, rows, slice(0, tx)) if f < total else packed(f - total, t)

    send_rows(at, total + more, ty, north_ref, south_ref)


def state_kernel(
    far_at,
    start,
    blocks,
    flag_ref,
    adj_ref,
    hist_ref,
    far_ref,
    diff_ref,
    mask_ref,
    west_ref,
    east_ref,
    north_ref,
    south_ref,
    mix_ref,
    coup_ref,
    out_ref,
    ring_ref,
    late_ref,
    state,
    force,
    spread,
):
    ty, tx = mask_ref.shape
    nc = adj_ref.shape[1]
    _, steps, fields = hist_ref.shape[:3]
    hw = steps
    per = LANES // hw
    ocean = flag_ref[0] == 0
    read, total = state_reader(adj_ref, hist_ref, far_ref, far_at, diff_ref, own_wet(flag_ref, mask_ref))
    wests, easts = sides_with_rows(west_ref, east_ref, north_ref, south_ref, total, start, blocks, tx)

    def ext(f):
        main = read(f, slice(0, ty), slice(0, tx))
        return with_ring(main, wests[f // per], easts[f // per], f, north_ref, south_ref, hw)

    for c in range(nc):
        state[c] = ext(c)
    forced = (steps - 1) * fields
    for k in range(1, steps):
        for q in range(fields):
            force[k, q] = ext(nc + (k - 1) * fields + q)
            force[k, fields + q] = ext(nc + forced + (k - 1) * fields + q)
    for q in range(fields):
        force[0, q, :ty, :tx] = hist_ref[0, 0, q]
        force[0, fields + q, :ty, :tx] = far_ref[far_at + q]
    diff, wet = ext(nc + 2 * forced), ext(nc + 2 * forced + 1)
    ring_ref[...] = diff
    ident = lax.broadcasted_iota(jnp.int32, (nc, nc), 0) == lax.broadcasted_iota(jnp.int32, (nc, nc), 1)
    step_m = mix_ref[0].T + ident.astype(F32)
    coup = coup_ref[0].T
    late = coup[:, fields:]
    powers = []
    for i in range(steps):
        powers.append(late)
        late = full_dot(step_m, late)
    columns = []
    for k in range(steps - 1, -1, -1):
        for j in range(k + 1):
            columns.append(math.comb(k, j) * powers[k - j])
    at = 0
    for column in columns:
        late_ref[:, at : at + fields * SUB] = grown(column)
        at += fields * SUB
    first = lax.broadcasted_iota(jnp.int32, coup.shape, 1) < fields
    coup = jnp.where(jnp.logical_or(first, ocean), coup, 0.0)
    mix8, coup8 = halves(grown(step_m)), stacked_rows(grown(coup))
    groups = ty // SUB
    main = [((g, 0, tx),) for g in range(groups)]
    halo = [((groups, 0, tx),)] + [
        tuple((g, tx, LANES) for g in range(at, min(at + tx // LANES, groups + 1)))
        for at in range(0, groups + 1, tx // LANES)
    ]

    for n in range(steps):
        k = steps - 1 - n
        small = n == steps - 1

        def one(c, carry):
            u = wet * state[c]
            state[c] = u
            spread[c] = ring_lap(diff * u)
            return carry

        lax.fori_loop(0, nc, one, 0, unroll=8)
        for places in main if small else main + halo:
            spots = [(slice(g * SUB, (g + 1) * SUB), slice(c, c + w)) for g, c, w in places]
            u = jnp.concatenate([state[:, rs, cs].reshape(nc * SUB, -1) for rs, cs in spots], axis=1)
            h = jnp.concatenate([force[k, :, rs, cs].reshape(2 * fields * SUB, -1) for rs, cs in spots], axis=1)
            new = dot3(mix8, halves(u)) + bf_dot(coup8, stacked_columns(h))
            at = 0
            for (rs, cs), (_, _, w) in zip(spots, places):
                value = new[:, at : at + w].reshape(nc, SUB, w) + spread[:, rs, cs]
                at += w
                if small:
                    out_ref[:, rs, cs] = value
                else:
                    state[:, rs, cs] = value


def late_fields(steps, fields):
    return [(n, q) for n in range(steps - 1) for q in range(fields)]


def late_main(steps, hf, own_ref, far_ref):
    def read(n, q):
        return far_ref[n * hf + q] if q < hf else own_ref[n * hf + q - hf]

    return read


def late_columns_kernel(steps, own_ref, far_ref, east_ref, west_ref):
    count, ty, tx = own_ref.shape
    hf = count // steps
    todo = late_fields(steps, 2 * hf)

    def read(f, l):
        n, q = todo[f]
        ref, i = (far_ref, n * hf + q) if q < hf else (own_ref, n * hf + q - hf)
        return ref[i, :, l * LANES : (l + 1) * LANES]

    east, west = pack_columns(read, len(todo), ty, tx, steps)
    for block, (e, w) in enumerate(zip(east, west)):
        east_ref[:, block * LANES : (block + 1) * LANES] = e
        west_ref[:, block * LANES : (block + 1) * LANES] = w


def late_rows_kernel(steps, blocks, own_ref, far_ref, west_ref, east_ref, north_ref, south_ref):
    count, ty, tx = own_ref.shape
    hf = count // steps
    todo = late_fields(steps, 2 * hf)
    packed, more = packed_reader(west_ref, east_ref, 0, blocks, tx)

    def read(f, t):
        if f >= len(todo):
            return packed(f - len(todo), t)
        n, q = todo[f]
        ref, i = (far_ref, n * hf + q) if q < hf else (own_ref, n * hf + q - hf)
        return ref[i, t * SUB : (t + 1) * SUB, :]

    send_rows(read, len(todo) + more, ty, north_ref, south_ref)


def late_kernel(
    steps,
    blocks,
    flag_ref,
    base_ref,
    ring_ref,
    late_ref,
    own_ref,
    far_ref,
    west_ref,
    east_ref,
    north_ref,
    south_ref,
    out_ref,
    stack,
):
    count, ty, tx = own_ref.shape
    hf = count // steps
    fields = 2 * hf
    nc = base_ref.shape[0]
    per = LANES // steps
    todo = late_fields(steps, fields)
    read = late_main(steps, hf, own_ref, far_ref)

    @pl.when(flag_ref[0] == 0)
    def _():
        out_ref[0] = base_ref[...]

    @pl.when(flag_ref[0] != 0)
    def _():
        diff = ring_ref[...]
        wests, easts = sides_with_rows(west_ref, east_ref, north_ref, south_ref, len(todo), 0, blocks, tx)
        at = 0
        for n in range(steps):
            k = steps - 1 - n
            for q in range(fields):
                r = read(n, q)
                if k:
                    f = todo.index((n, q))
                    r = with_ring(r, wests[f // per], easts[f // per], f, north_ref, south_ref, steps)
                for j in range(k + 1):
                    stack[at + j * fields + q] = r[:ty, :tx]
                    if j < k:
                        r = ring_lap(diff * r)
            at += (k + 1) * fields
        big = halves(late_ref[...])
        for g in range(ty // SUB):
            for l in range(tx // LANES):
                rs, cs = slice(g * SUB, (g + 1) * SUB), slice(l * LANES, (l + 1) * LANES)
                more = dot3(big, halves(stack[:, rs, cs].reshape(-1, LANES)))
                out_ref[0, :, rs, cs] = base_ref[:, rs, cs] + more.reshape(nc, SUB, LANES)


def shifted(x, axis, by, wrap, sect=None):
    size = lax.axis_size(axis)
    pairs = [(i, (i + by) % size) for i in range(size) if wrap or 0 <= i + by < size]
    if sect is None:
        return lax.ppermute(x, axis, pairs)
    base = sect * size
    return lax.ppermute(x, ("sect", axis), [(base + i, base + j) for i, j in pairs])


def struct(*shape):
    return jax.ShapeDtypeStruct(shape, F32)


def partial(kernel, *args):
    def run(*refs):
        kernel(*args, *refs)

    run.__name__ = kernel.__name__
    return run


def body(
    adjoint_init,
    diffusivity,
    mixing,
    coupling,
    history,
    extract,
    land_mask,
    regrid,
    atmos_tile_index,
    ocean_block_index,
    atmos_block_index,
):
    _, steps, fields, ty, tx = history.shape
    nc = adjoint_init.shape[1]
    hf, hw = fields // 2, steps
    per = LANES // hw
    sect = lax.axis_index("sect").astype(jnp.int32)
    tile = (lax.axis_index("gy") * lax.axis_size("gx") + lax.axis_index("gx")).astype(jnp.int32)
    flag = sect.reshape(1)
    tiles = lax.axis_size("gy") * lax.axis_size("gx")
    entries = ocean_block_index.shape[0] // tiles
    cap = 2 * entries // tiles
    cells = regrid.shape[1]
    slots = ty * tx // cells
    nb = tx // cells

    def exchange(x_after, x_before, axis, wrap, only=None):
        return shifted(x_after, axis, 1, wrap, only), shifted(x_before, axis, -1, wrap, only)

    count = (steps + 1) * hf
    coupling = jnp.swapaxes(coupling, 1, 2)
    keep, send = call(
        project_kernel,
        [struct(count + 1, ty, tx), struct(count + 2 + steps * fields, ty, tx)],
        adjoint_init, land_mask, diffusivity, history, mixing, extract, coupling,
        hbm=(0, 1, 2, 3),
        vmem=60,
        scratch=[
            pltpu.VMEM((nc, ty, tx), F32),
            pltpu.VMEM((ty, tx), jnp.int32),
            pltpu.SemaphoreType.DMA((3 + steps,)),
        ],
    )
    got = lax.ppermute(send, "sect", [(0, 1), (1, 0)])
    places, halo_count = field_places(steps, hf)
    blocks = -(-halo_count // per)
    far_at = count + 2
    total = nc + 2 * (steps - 1) * fields + 2
    state_blocks = -(-total // per)
    side = struct(ty, (blocks + state_blocks) * LANES)
    main, east, west = call(
        partial(force_kernel, places, halo_count),
        [struct(len(places), ty, tx), side, side],
        flag, keep, got, adjoint_init, history, diffusivity, land_mask,
        smem=(0,),
    )
    from_west, from_east = exchange(east, west, "gx", True)
    pairs = -(-(halo_count + -(-2 * blocks * LANES // tx)) // 2)
    north, south = call(
        partial(rows_kernel, halo_count, blocks),
        [struct(pairs, SUB, tx)] * 2,
        main, from_west, from_east,
    )
    from_north, from_south = exchange(south, north, "gy", False)
    dest = atmos_tile_index.reshape(tiles, entries)
    [sel] = call(
        partial(select_kernel, cap, slots, nb),
        [struct(tiles * cap, slots)],
        tile.reshape(1), dest, ocean_block_index.reshape(tiles, entries),
        smem=(0,),
    )
    [packed] = call(
        partial(surface_kernel, places, halo_count, steps, hf),
        [struct(tiles * cap, steps * hf * LANES)],
        main, from_west, from_east, from_north, from_south, regrid, sel,
    )
    packed, adjoint_init, dest = lax.optimization_barrier((packed, adjoint_init, dest))
    arrived = lax.all_to_all(
        packed.reshape(tiles, cap, -1), ("gy", "gx"), split_axis=0, concat_axis=0, tiled=True
    ).reshape(tiles * cap, -1)

    pairs = -(-(total + -(-2 * state_blocks * LANES // tx)) // 2)
    north, south = call(
        partial(state_rows_kernel, far_at, blocks, state_blocks),
        [struct(pairs, SUB, tx)] * 2,
        flag, adjoint_init, history, got, diffusivity, land_mask, from_west, from_east,
        smem=(0,),
    )
    from_north, from_south = exchange(south, north, "gy", False)
    terms = fields * steps * (steps + 1) // 2
    ext = (ty + SUB, tx + LANES)
    base, ring, late = call(
        partial(state_kernel, far_at, blocks, state_blocks),
        [struct(nc, ty, tx), struct(*ext), struct(nc * SUB, terms * SUB)],
        flag, adjoint_init, history, got, diffusivity, land_mask,
        from_west, from_east, from_north, from_south, mixing, coupling,
        smem=(0,),
        scratch=[
            pltpu.VMEM((nc, *ext), F32),
            pltpu.VMEM((steps, 2 * fields, *ext), F32),
            pltpu.VMEM((nc, *ext), F32),
        ],
    )

    [acc] = call(
        partial(arrival_kernel, cap, slots, nb),
        [struct(slots, tiles * cap)],
        tile.reshape(1), dest, atmos_block_index.reshape(tiles, entries),
        smem=(0,),
    )
    arrived, base, acc = lax.optimization_barrier((arrived, base, acc))
    [own] = call(gather_kernel, [struct(steps * hf, ty, tx)], acc, arrived)
    far = lax.ppermute(own, "sect", [(0, 1)])
    halo_count = (steps - 1) * fields
    blocks = -(-halo_count // per)
    east, west = call(partial(late_columns_kernel, steps), [struct(ty, blocks * LANES)] * 2, own, far)
    from_west, from_east = exchange(east, west, "gx", True, 1)
    pairs = -(-(halo_count + -(-2 * blocks * LANES // tx)) // 2)
    north, south = call(
        partial(late_rows_kernel, steps, blocks), [struct(pairs, SUB, tx)] * 2, own, far, from_west, from_east
    )
    from_north, from_south = exchange(south, north, "gy", False, 1)
    [out] = call(
        partial(late_kernel, steps, blocks),
        [struct(1, nc, ty, tx)],
        flag, base, ring, late, own, far, from_west, from_east, from_north, from_south,
        smem=(0,),
        scratch=[pltpu.VMEM((terms, ty, tx), F32)],
    )
    return out


def solution(mesh):
    placed = (
        P("sect", None, "gy", "gx"),
        P("sect", "gy", "gx"),
        P("sect", None, None),
        P("sect", None, None),
        P("sect", None, None, "gy", "gx"),
        P(),
        P("gy", "gx"),
        P(("gy", "gx"), None, None),
        P(),
        P(),
        P(),
    )
    return jax.shard_map(
        body, mesh=mesh, in_specs=placed, out_specs=P("sect", None, "gy", "gx"), check_vma=False
    )
```

```python
import math

import jax
import jax.numpy as jnp
from jax import lax
from jax.experimental import pallas as pl
from jax.experimental.pallas import tpu as pltpu
from jax.sharding import PartitionSpec as P

LANES = 128
SUB = 8
F32 = jnp.float32
BF16 = jnp.bfloat16


LAST = (((1,), (1,)), ((), ()))


def full_dot(a, b, dims=(((1,), (0,)), ((), ()))):
    return lax.dot_general(a, b, dims, precision=lax.Precision.HIGHEST, preferred_element_type=F32)


def halves(x):
    high = x.astype(BF16)
    return high, (x - high.astype(F32)).astype(BF16)


def bf_dot(a, b, dims=(((1,), (0,)), ((), ()))):
    return lax.dot_general(a, b, dims, preferred_element_type=F32)


def dot3(a, b):
    (ah, al), (bh, bl) = a, b
    return bf_dot(ah, bh) + (bf_dot(ah, bl) + bf_dot(al, bh))


def grown(matrix):
    rows, cols = matrix.shape
    up = lax.broadcasted_iota(jnp.int32, (rows * SUB, rows), 0) // SUB
    up = (up == lax.broadcasted_iota(jnp.int32, (rows * SUB, rows), 1)).astype(F32)
    out = lax.broadcasted_iota(jnp.int32, (cols, cols * SUB), 1) // SUB
    out = (out == lax.broadcasted_iota(jnp.int32, (cols, cols * SUB), 0)).astype(F32)
    spread = full_dot(full_dot(up, matrix), out)
    i = lax.broadcasted_iota(jnp.int32, spread.shape, 0) % SUB
    j = lax.broadcasted_iota(jnp.int32, spread.shape, 1) % SUB
    return jnp.where(i == j, spread, 0.0)


def lane_ids(rows):
    return lax.broadcasted_iota(jnp.int32, (rows, LANES), 1)


def pack_columns(read, count, rows, tx, hw):
    per = LANES // hw
    ids = lane_ids(rows) // hw
    east, west = [], []
    last = tx // LANES - 1
    for block in range(-(-count // per)):
        e = jnp.zeros((rows, LANES), F32)
        w = jnp.zeros((rows, LANES), F32)
        for place in range(min(per, count - block * per)):
            f = block * per + place
            e_in, w_in = read(f, last), read(f, 0)
            e_shift, w_shift = (place * hw + hw) % LANES, place * hw
            e_in = pltpu.roll(e_in, e_shift, 1) if e_shift else e_in
            w_in = pltpu.roll(w_in, w_shift, 1) if w_shift else w_in
            e = jnp.where(ids == place, e_in, e)
            w = jnp.where(ids == place, w_in, w)
        east.append(e)
        west.append(w)
    return east, west


def store_columns(read, count, tx, hw, east_ref, west_ref, start):
    east, west = pack_columns(read, count, east_ref.shape[0], tx, hw)
    for block, (e, w) in enumerate(zip(east, west)):
        east_ref[:, (start + block) * LANES : (start + block + 1) * LANES] = e
        west_ref[:, (start + block) * LANES : (start + block + 1) * LANES] = w


def side_block(from_west, from_east, f, hw):
    place = f % (LANES // hw)
    ids = lane_ids(from_west.shape[0])
    e_shift, w_shift = (-place * hw) % LANES, (-hw - place * hw) % LANES
    e = pltpu.roll(from_east, e_shift, 1) if e_shift else from_east
    w = pltpu.roll(from_west, w_shift, 1) if w_shift else from_west
    return jnp.where(ids < hw, e, jnp.where(ids >= LANES - hw, w, 0.0))


def strip_places(widths):
    used, spots = [], [None] * len(widths)
    for f in sorted(range(len(widths)), key=lambda f: -widths[f]):
        t = next((t for t, rows in enumerate(used) if rows + widths[f] <= SUB), len(used))
        if t == len(used):
            used.append(0)
        spots[f] = (t, used[t])
        used[t] += widths[f]
    return spots, len(used)


def turn(x, by):
    return pltpu.roll(x, by % SUB, 0) if by % SUB else x


def edge_reader(north_ref, south_ref, widths):
    spots, _ = strip_places(widths)

    def edge(f, cols=slice(None)):
        (t, first), w = spots[f], widths[f]
        south = turn(south_ref[t, :, cols], -first)
        north = turn(north_ref[t, :, cols], -w - first)
        sub = lax.broadcasted_iota(jnp.int32, south.shape, 0)
        return jnp.where(sub < w, south, jnp.where(sub >= SUB - w, north, 0.0))

    return edge


def send_rows(read, widths, ty, north_ref, south_ref):
    spots, tiles = strip_places(widths)
    last = ty // SUB - 1
    sub = lax.broadcasted_iota(jnp.int32, north_ref.shape[1:], 0)
    for t in range(tiles):
        north = south = jnp.zeros(north_ref.shape[1:], F32)
        for f, (at, first) in enumerate(spots):
            if at == t:
                here = (sub >= first) & (sub < first + widths[f])
                north = jnp.where(here, turn(read(f, 0), first), north)
                south = jnp.where(here, turn(read(f, last), first + widths[f]), south)
        north_ref[t] = north
        south_ref[t] = south


def ring_lap(p):
    rows, cols = p.shape
    around = pltpu.roll(p, 1, 0) + pltpu.roll(p, rows - 1, 0)
    around = around + pltpu.roll(p, 1, 1) + pltpu.roll(p, cols - 1, 1)
    return around - 4.0 * p


def with_ring(main, packed_west, packed_east, f, edge, hw):
    bottom = edge(f)
    side = side_block(packed_west, packed_east, f, hw)
    return jnp.concatenate([jnp.concatenate([main, bottom], axis=0), side], axis=1)


def sides_with_rows(west_ref, east_ref, edge, first, start, blocks, tx):
    west, east = [], []
    per = tx // LANES
    for block in range(blocks):
        out = []
        for which, ref in enumerate((west_ref, east_ref)):
            f, at = divmod(which * blocks + block, per)
            tile = edge(first + f, slice(at * LANES, (at + 1) * LANES))
            out.append(jnp.concatenate([ref[:, pl.ds((start + block) * LANES, LANES)], tile], axis=0))
        west.append(out[0])
        east.append(out[1])
    return west, east


def packed_reader(west_ref, east_ref, start, blocks, tx):
    per = tx // LANES

    def read(f, row_tile):
        pieces = []
        for at in range(per):
            which, block = divmod(f * per + at, blocks)
            rows = pl.ds(row_tile * SUB, SUB)
            if which < 2:
                pieces.append((west_ref, east_ref)[which][rows, pl.ds((start + block) * LANES, LANES)])
            else:
                pieces.append(jnp.zeros((SUB, LANES), F32))
        return jnp.concatenate(pieces, axis=1)

    return read, -(-2 * blocks // per)


def with_packed(widths, blocks, tx, hw):
    return widths + [hw] * -(-2 * blocks * LANES // tx)


def projected_widths(places, halo_count, steps):
    widths = [0] * halo_count
    for key, f in places.items():
        if f < halo_count:
            widths[f] = steps if key == "d" else steps - 1 if key == "w" else steps - key[1] if key[0] == "t" else steps - 1 - key[1] - key[2]
    return widths


def state_widths(steps, fields, nc):
    return [k for _ in range(2) for k in range(1, steps) for _ in range(fields)] + [steps] * (2 + nc)


def late_widths(steps, fields):
    return [steps - 1 - n for n, _ in late_fields(steps, fields)]


def call(kernel, outs, *args, smem=(), hbm=(), hbm_out=False, scratch=(), flops=0):
    space = lambda i: pltpu.SMEM if i in smem else pltpu.HBM if i in hbm else pltpu.VMEM
    args = [pltpu.with_memory_space_constraint(a, pltpu.HBM) if i in hbm else a for i, a in enumerate(args)]
    nbytes = sum(math.prod(a.shape) * 4 for a in (*args, *outs))
    return pl.pallas_call(
        kernel,
        out_shape=[pltpu.HBM(o.shape, o.dtype) for o in outs] if hbm_out else outs,
        in_specs=[pl.BlockSpec(memory_space=space(i)) for i in range(len(args))],
        out_specs=[pl.BlockSpec(memory_space=pltpu.HBM if hbm_out else pltpu.VMEM) for _ in outs],
        scratch_shapes=scratch,
        compiler_params=pltpu.CompilerParams(vmem_limit_bytes=48 * 2**20),
        cost_estimate=pl.CostEstimate(flops=flops, bytes_accessed=nbytes, transcendentals=0),
    )(*args)


def stacked_rows(parts):
    high, low = halves(parts)
    return jnp.concatenate([high, high, low], axis=1)


def stacked_columns(parts):
    high, low = halves(parts)
    return jnp.concatenate([high, low, high], axis=0)


def project_kernel(
    adj_hbm, mask_hbm, diff_hbm, hist_hbm, mix_hbm, ext_hbm, coup_hbm,
    keep_ref, send_ref, east_ref, west_ref, adj_ref, mask_ref, mix_ref, ext_ref, coup_ref, chain_ref, sems,
):
    _, nc, ty, tx = adj_hbm.shape
    _, steps, fields = hist_hbm.shape[:3]
    hf = fields // 2
    count = (steps + 1) * hf
    copies = [
        pltpu.make_async_copy(mask_hbm, mask_ref, sems.at[0]),
        pltpu.make_async_copy(adj_hbm.at[0], adj_ref, sems.at[1]),
        pltpu.make_async_copy(diff_hbm.at[0], send_ref.at[count + 1], sems.at[2]),
    ]
    for k in range(steps):
        to = send_ref.at[pl.ds(count + 2 + k * fields, fields)]
        copies.append(pltpu.make_async_copy(hist_hbm.at[0, k], to, sems.at[3 + k]))
    small = [
        pltpu.make_async_copy(a, b, sems.at[3 + steps + i])
        for i, (a, b) in enumerate(((mix_hbm, mix_ref), (ext_hbm, ext_ref), (coup_hbm, coup_ref)))
    ]
    for copy in small + copies:
        copy.start()
    for copy in small:
        copy.wait()
    mix = mix_ref[0]
    rows = ext_ref[...]
    chain_ref[...] = jnp.zeros_like(chain_ref)
    for m in range(steps + 1):
        chain_ref[m * fields : (m + 1) * fields, :] = rows
        rows = rows + full_dot(rows, mix, LAST)
    chain = chain_ref[...]
    big = grown(chain)
    half = lambda x, h: jnp.concatenate(
        [x[(m * fields + h * hf) * SUB : (m * fields + (h + 1) * hf) * SUB] for m in range(steps + 1)], axis=0
    )
    force = grown(full_dot(chain, coup_ref[0], LAST))
    height, width = hf * SUB, force.shape[1]
    for m in range(steps):
        for h, ref in enumerate((keep_ref, send_ref)):
            per = ty // height
            r0, c0 = (m % per) * height, (m // per) * LANES
            at = (m * fields + h * hf) * SUB
            ref[count, r0 : r0 + height, c0 : c0 + width] = force[at : at + height]
    big = halves(jnp.concatenate([half(big, 0), half(big, 1)], axis=0))
    copies[0].wait()
    copies[1].wait()
    wet = mask_ref[...].astype(F32)
    keep_ref[count + 1] = wet
    for g in range(ty // SUB):
        rs = slice(g * SUB, (g + 1) * SUB)
        u = (adj_ref[:, rs, :] * wet[rs][None]).reshape(nc * SUB, tx)
        t = dot3(big, halves(u)).reshape(2 * count, SUB, tx)
        keep_ref[:count, rs, :] = t[:count]
        send_ref[:count, rs, :] = t[count:]
    store_columns(lambda f, l: adj_ref[f, :, l * LANES : (l + 1) * LANES], nc, tx, steps, east_ref, west_ref, 0)
    for copy in copies[2:]:
        copy.wait()


def field_places(steps, hf):
    with_halo, without = [], []
    for m in range(steps + 1):
        for q in range(hf):
            (with_halo if m < steps else without).append(("t", m, q))
    for n in range(steps):
        for m in range(steps - n):
            for q in range(hf):
                (with_halo if n + m < steps - 1 else without).append(("g", n, m, q))
    with_halo += ["d", "w"]
    return {key: i for i, key in enumerate(with_halo + without)}, len(with_halo)


def force_kernel(
    places, halo_count, steps, fields, flag_ref, keep_ref, send_ref, got_ref, adj_east_ref, adj_west_ref,
    main_ref, east_ref, west_ref,
):
    _, ty, tx = main_ref.shape
    hf, hw = fields // 2, steps
    count = (steps + 1) * hf
    ocean = flag_ref[0] == 0
    pick = lambda a, b: jnp.where(ocean, a, b)
    for m in range(steps + 1):
        for q in range(hf):
            main_ref[places["t", m, q]] = pick(keep_ref[m * hf + q], got_ref[m * hf + q])
    main_ref[places["d"]] = pick(send_ref[count + 1], got_ref[count + 1])
    main_ref[places["w"]] = keep_ref[count + 1]
    height, width = hf * SUB, 2 * fields * SUB
    per = ty // height
    big = []
    for m in range(steps):
        r0, c0 = (m % per) * height, (m // per) * LANES
        at = (count, slice(r0, r0 + height), slice(c0, c0 + width))
        big.append(pick(keep_ref[at], got_ref[at]))
    big = stacked_rows(jnp.concatenate(big, axis=0))
    for g in range(ty // SUB):
        rs = slice(g * SUB, (g + 1) * SUB)
        for n in range(steps):
            k = steps - 1 - n
            at = (slice(count + 2 + k * fields, count + 2 + (k + 1) * fields), rs)
            own, far = send_ref[at], got_ref[at]
            h = jnp.concatenate([pick(own, far), pick(far, own)], axis=0).reshape(-1, tx)
            out = bf_dot(big[: (steps - n) * height], stacked_columns(h))
            for m in range(steps - n):
                for q in range(hf):
                    at = (m * hf + q) * SUB
                    main_ref[places["g", n, m, q], rs, :] = out[at : at + SUB]
    read = lambda f, l: main_ref[f, :, l * LANES : (l + 1) * LANES]
    store_columns(read, halo_count, tx, hw, east_ref, west_ref, 0)
    start = -(-halo_count // (LANES // hw))
    state, total = forced_reader(steps, fields, flag_ref, send_ref, got_ref, keep_ref)
    read = lambda f, l: state(f, slice(0, ty), slice(l * LANES, (l + 1) * LANES))
    store_columns(read, total, tx, hw, east_ref, west_ref, start)
    start += -(-total // (LANES // hw))
    east_ref[:, start * LANES :] = adj_east_ref[...]
    west_ref[:, start * LANES :] = adj_west_ref[...]


def rows_kernel(widths, blocks, main_ref, west_ref, east_ref, north_ref, south_ref):
    _, ty, tx = main_ref.shape
    packed, more = packed_reader(west_ref, east_ref, 0, blocks, tx)
    count = len(widths) - more

    def read(f, t):
        return main_ref[f, t * SUB : (t + 1) * SUB, :] if f < count else packed(f - count, t)

    send_rows(read, widths, ty, north_ref, south_ref)


def block_place(slots, nb):
    return lambda b: (b % nb) * (slots // nb) + b // nb


def onehot(size, values):
    ids = lax.broadcasted_iota(jnp.int32, (size, values.shape[1]), 0)
    return (ids == values).astype(F32).astype(BF16)


def earlier(entries):
    row = lax.broadcasted_iota(jnp.int32, (entries, entries), 0)
    return row < lax.broadcasted_iota(jnp.int32, (entries, entries), 1)


def select_kernel(cap, slots, nb, pos_ref, dest_ref, src_ref, regrid_ref, sel_ref, weights_ref):
    tiles, entries = dest_ref.shape
    tile = pos_ref[0]
    dest = dest_ref[pl.ds(tile, 1), :]
    across = jnp.broadcast_to(dest.astype(F32), (entries, entries))
    same = (across == across.T) & earlier(entries)
    rank = jnp.sum(same.astype(F32), axis=0, keepdims=True).astype(jnp.int32)
    source = block_place(slots, nb)(src_ref[pl.ds(tile, 1), :])
    weights_ref[...] = regrid_ref[0]
    sel_ref[...] = bf_dot(onehot(tiles * cap, dest * cap + rank), onehot(slots, source), LAST)


def arrival_kernel(cap, slots, nb, pos_ref, dest_ref, dst_ref, acc_ref):
    tiles, entries = dest_ref.shape
    tile = pos_ref[0]
    acc_ref[...] = jnp.zeros_like(acc_ref)
    before = earlier(entries).astype(F32).astype(BF16)

    def source(i, carry):
        mine = dest_ref[pl.ds(i, 1), :] == tile
        mine_f = jnp.broadcast_to(mine.astype(F32), (SUB, entries)).astype(BF16)
        ranks = bf_dot(mine_f, before)[:1].astype(jnp.int32)
        spot = jnp.where(mine, i * cap + ranks, -1)
        place = block_place(slots, nb)(dst_ref[pl.ds(i, 1), :])
        acc_ref[...] += bf_dot(onehot(slots, place), onehot(tiles * cap, spot), LAST)
        return carry

    lax.fori_loop(0, tiles, source, 0, unroll=4)


def surface_kernel(
    places, halo_count, widths, steps, hf, main_ref, west_ref, east_ref, north_ref, south_ref, weights_ref, sel_ref,
    out_hbm, out_ref, sems,
):
    _, ty, tx = main_ref.shape
    hw = steps
    per = LANES // hw
    blocks = -(-halo_count // per)
    edge = edge_reader(north_ref, south_ref, widths)
    wests, easts = sides_with_rows(west_ref, east_ref, edge, halo_count, 0, blocks, tx)

    def ext(key):
        f = places[key]
        if f < halo_count:
            return with_ring(main_ref[f], wests[f // per], easts[f // per], f, edge, hw)
        main = jnp.concatenate([main_ref[f], jnp.zeros((SUB, tx), F32)], axis=0)
        return jnp.concatenate([main, jnp.zeros((ty + SUB, LANES), F32)], axis=1)

    diff, wet = ext("d"), ext("w")
    weights = halves(weights_ref[...])
    sel = sel_ref[...].astype(BF16)
    copies = []
    for q in range(hf):
        t = [ext(("t", m, q)) for m in range(steps + 1)]
        for n in range(steps):
            t = [wet * (t[m + 1] + ring_lap(diff * t[m]) + ext(("g", n, m, q))) for m in range(steps - n)]
            s = jnp.concatenate([t[0][:ty, l * LANES : (l + 1) * LANES] for l in range(tx // LANES)], axis=0)
            s = halves(dot3(halves(s), weights))
            at = (n * hf + q) * LANES
            out_ref[:, at : at + LANES] = bf_dot(sel, s[0]) + bf_dot(sel, s[1])
            to = out_hbm.at[:, pl.ds(at, LANES)]
            copies.append(pltpu.make_async_copy(out_ref.at[:, pl.ds(at, LANES)], to, sems.at[n * hf + q]))
            copies[-1].start()
    for copy in copies:
        copy.wait()


def gather_kernel(acc_ref, in_ref, after_ref, out_ref):
    count, ty, tx = out_ref.shape
    acc = acc_ref[...].astype(BF16)
    for i in range(count):
        high, low = halves(in_ref[:, i * LANES : (i + 1) * LANES])
        total = bf_dot(acc, high) + bf_dot(acc, low)
        for l in range(tx // LANES):
            out_ref[i, :, l * LANES : (l + 1) * LANES] = total[l * ty : (l + 1) * ty]


def forced_reader(steps, fields, flag_ref, send_ref, got_ref, keep_ref):
    count = (steps + 1) * (fields // 2)
    forced = (steps - 1) * fields

    def read(f, rows, cols):
        if f < 2 * forced:
            part, f = divmod(f, forced)
            return (send_ref, got_ref)[part][count + 2 + fields + f, rows, cols]
        if f == 2 * forced:
            return send_ref[count + 1, rows, cols]
        return jnp.where(flag_ref[0] == 0, keep_ref[count + 1, rows, cols], 1.0)

    return read, 2 * forced + 2


def state_rows_kernel(
    steps, fields, start, blocks, flag_ref, adj_hbm, send_ref, got_ref, keep_ref, west_ref, east_ref,
    north_ref, south_ref, edges, sems,
):
    _, nc, ty, tx = adj_hbm.shape
    copies = [
        pltpu.make_async_copy(adj_hbm.at[0, :, pl.ds(t, SUB), :], edges.at[i], sems.at[i])
        for i, t in enumerate((0, ty - SUB))
    ]
    for copy in copies:
        copy.start()
    forced, total = forced_reader(steps, fields, flag_ref, send_ref, got_ref, keep_ref)
    packed, _ = packed_reader(west_ref, east_ref, start, blocks, tx)
    for copy in copies:
        copy.wait()

    def read(f, t):
        if f < total:
            return forced(f, slice(t * SUB, (t + 1) * SUB), slice(0, tx))
        f -= total
        return edges[min(t, 1), f] if f < nc else packed(f - nc, t)

    widths = with_packed(state_widths(steps, fields, nc), blocks, tx, steps)
    send_rows(read, widths, ty, north_ref, south_ref)


def matrices_kernel(steps, fields, flag_ref, mix_ref, coup_ref, mix8_ref, coup8_ref, late_ref):
    nc = mix_ref.shape[1]
    ident = lax.broadcasted_iota(jnp.int32, (nc, nc), 0) == lax.broadcasted_iota(jnp.int32, (nc, nc), 1)
    step_m = mix_ref[0].T + ident.astype(F32)
    coup = coup_ref[0].T
    late = coup[:, fields:]
    powers = []
    for i in range(steps):
        powers.append(late)
        late = full_dot(step_m, late)
    at = 0
    for k in range(steps - 1, -1, -1):
        for j in range(k + 1):
            late_ref[:, at : at + fields * SUB] = grown(math.comb(k, j) * powers[k - j])
            at += fields * SUB
    first = lax.broadcasted_iota(jnp.int32, coup.shape, 1) < fields
    mix8_ref[...] = grown(step_m)
    coup8_ref[...] = grown(jnp.where(jnp.logical_or(first, flag_ref[0] == 0), coup, 0.0))


def state_kernel(
    steps, fields, start, blocks, flag_ref, adj_hbm, send_ref, got_ref, keep_ref, west_ref, east_ref, north_ref,
    south_ref, mix8_ref, coup8_ref, out_ref, ring_ref, state, force, spread, sem,
):
    _, nc, ty, tx = adj_hbm.shape
    copy = pltpu.make_async_copy(adj_hbm.at[0], out_ref, sem)
    copy.start()
    hw = steps
    per = LANES // hw
    read, total = forced_reader(steps, fields, flag_ref, send_ref, got_ref, keep_ref)
    edge = edge_reader(north_ref, south_ref, with_packed(state_widths(steps, fields, nc), blocks, tx, hw))
    wests, easts = sides_with_rows(west_ref, east_ref, edge, total + nc, start, blocks, tx)

    def ext(f):
        main = read(f, slice(0, ty), slice(0, tx))
        return with_ring(main, wests[f // per], easts[f // per], f, edge, hw)

    forced = (steps - 1) * fields
    for k in range(1, steps):
        for q in range(fields):
            force[k, q] = ext((k - 1) * fields + q)
            force[k, fields + q] = ext(forced + (k - 1) * fields + q)
    at = (steps + 1) * (fields // 2) + 2
    for q in range(fields):
        force[0, q, :ty, :tx] = send_ref[at + q]
        force[0, fields + q, :ty, :tx] = got_ref[at + q]
    diff, wet = ext(2 * forced), ext(2 * forced + 1)
    ring_ref[...] = diff
    mix8, coup8 = halves(mix8_ref[...]), stacked_rows(coup8_ref[...])
    groups = ty // SUB
    main = [((g, 0, tx),) for g in range(groups)]
    halo = [((groups, 0, tx),)] + [
        tuple((g, tx, LANES) for g in range(at, min(at + tx // LANES, groups + 1)))
        for at in range(0, groups + 1, tx // LANES)
    ]
    copy.wait()
    block = -(-total // per)
    for c in range(nc):
        west, east = wests[block + c // per], easts[block + c // per]
        state[c, :ty, :tx] = out_ref[c]
        state[c, ty:, :tx] = edge(total + c)
        state[c, :, tx:] = side_block(west, east, c, hw)

    for n in range(steps):
        k = steps - 1 - n
        small = n == steps - 1

        def one(c, carry):
            u = wet * state[c]
            state[c] = u
            spread[c] = ring_lap(diff * u)
            return carry

        lax.fori_loop(0, nc, one, 0, unroll=8)
        for places in main if small else main + halo:
            spots = [(slice(g * SUB, (g + 1) * SUB), slice(c, c + w)) for g, c, w in places]
            u = jnp.concatenate([state[:, rs, cs].reshape(nc * SUB, -1) for rs, cs in spots], axis=1)
            h = jnp.concatenate([force[k, :, rs, cs].reshape(2 * fields * SUB, -1) for rs, cs in spots], axis=1)
            new = dot3(mix8, halves(u)) + bf_dot(coup8, stacked_columns(h))
            at = 0
            for (rs, cs), (_, _, w) in zip(spots, places):
                value = new[:, at : at + w].reshape(nc, SUB, w) + spread[:, rs, cs]
                at += w
                if small:
                    out_ref[:, rs, cs] = value
                else:
                    state[:, rs, cs] = value


def late_fields(steps, fields):
    return [(n, q) for n in range(steps - 1) for q in range(fields)]


def late_main(steps, hf, own_ref, far_ref):
    def read(n, q):
        return far_ref[n * hf + q] if q < hf else own_ref[n * hf + q - hf]

    return read


def late_columns_kernel(steps, own_ref, far_ref, east_ref, west_ref):
    count, ty, tx = own_ref.shape
    hf = count // steps
    todo = late_fields(steps, 2 * hf)

    def read(f, l):
        n, q = todo[f]
        ref, i = (far_ref, n * hf + q) if q < hf else (own_ref, n * hf + q - hf)
        return ref[i, :, l * LANES : (l + 1) * LANES]

    east, west = pack_columns(read, len(todo), ty, tx, steps)
    for block, (e, w) in enumerate(zip(east, west)):
        east_ref[:, block * LANES : (block + 1) * LANES] = e
        west_ref[:, block * LANES : (block + 1) * LANES] = w


def late_rows_kernel(steps, blocks, own_ref, far_ref, west_ref, east_ref, north_ref, south_ref):
    count, ty, tx = own_ref.shape
    hf = count // steps
    todo = late_fields(steps, 2 * hf)
    packed, _ = packed_reader(west_ref, east_ref, 0, blocks, tx)

    def read(f, t):
        if f >= len(todo):
            return packed(f - len(todo), t)
        n, q = todo[f]
        ref, i = (far_ref, n * hf + q) if q < hf else (own_ref, n * hf + q - hf)
        return ref[i, t * SUB : (t + 1) * SUB, :]

    send_rows(read, with_packed(late_widths(steps, 2 * hf), blocks, tx, steps), ty, north_ref, south_ref)


def late_kernel(
    steps,
    blocks,
    flag_ref,
    base_ref,
    ring_ref,
    late_ref,
    own_ref,
    far_ref,
    west_ref,
    east_ref,
    north_ref,
    south_ref,
    out_ref,
    stack,
):
    count, ty, tx = own_ref.shape
    hf = count // steps
    fields = 2 * hf
    nc = base_ref.shape[0]
    per = LANES // steps
    todo = late_fields(steps, fields)
    read = late_main(steps, hf, own_ref, far_ref)

    @pl.when(flag_ref[0] == 0)
    def _():
        out_ref[0] = base_ref[...]

    @pl.when(flag_ref[0] != 0)
    def _():
        diff = ring_ref[...]
        edge = edge_reader(north_ref, south_ref, with_packed(late_widths(steps, fields), blocks, tx, steps))
        wests, easts = sides_with_rows(west_ref, east_ref, edge, len(todo), 0, blocks, tx)
        at = 0
        for n in range(steps):
            k = steps - 1 - n
            for q in range(fields):
                r = read(n, q)
                if k:
                    f = todo.index((n, q))
                    r = with_ring(r, wests[f // per], easts[f // per], f, edge, steps)
                for j in range(k + 1):
                    stack[at + j * fields + q] = r[:ty, :tx]
                    if j < k:
                        r = ring_lap(diff * r)
            at += (k + 1) * fields
        big = halves(late_ref[...])
        for g in range(ty // SUB):
            for l in range(tx // LANES):
                rs, cs = slice(g * SUB, (g + 1) * SUB), slice(l * LANES, (l + 1) * LANES)
                more = dot3(big, halves(stack[:, rs, cs].reshape(-1, LANES)))
                out_ref[0, :, rs, cs] = base_ref[:, rs, cs] + more.reshape(nc, SUB, LANES)


def shifted(x, axis, by, wrap, sect=None):
    size = lax.axis_size(axis)
    pairs = [(i, (i + by) % size) for i in range(size) if wrap or 0 <= i + by < size]
    if sect is None:
        return lax.ppermute(x, axis, pairs)
    base = sect * size
    return lax.ppermute(x, ("sect", axis), [(base + i, base + j) for i, j in pairs])


def struct(*shape):
    return jax.ShapeDtypeStruct(shape, F32)


def partial(kernel, *args):
    def run(*refs):
        kernel(*args, *refs)

    run.__name__ = kernel.__name__
    return run


def body(
    adjoint_init,
    diffusivity,
    mixing,
    coupling,
    history,
    extract,
    land_mask,
    regrid,
    atmos_tile_index,
    ocean_block_index,
    atmos_block_index,
):
    _, steps, fields, ty, tx = history.shape
    nc = adjoint_init.shape[1]
    hf, hw = fields // 2, steps
    per = LANES // hw
    sect = lax.axis_index("sect").astype(jnp.int32)
    tile = (lax.axis_index("gy") * lax.axis_size("gx") + lax.axis_index("gx")).astype(jnp.int32)
    flag = sect.reshape(1)
    tiles = lax.axis_size("gy") * lax.axis_size("gx")
    entries = ocean_block_index.shape[0] // tiles
    cap = 2 * entries // tiles
    cells = regrid.shape[1]
    slots = ty * tx // cells
    nb = tx // cells

    def exchange(x_after, x_before, axis, wrap, only=None):
        return shifted(x_after, axis, 1, wrap, only), shifted(x_before, axis, -1, wrap, only)

    count = (steps + 1) * hf
    coupling = jnp.swapaxes(coupling, 1, 2)
    columns = struct(ty, -(-nc // per) * LANES)
    keep, send, east, west = call(
        project_kernel,
        [struct(count + 2, ty, tx), struct(count + 2 + steps * fields, ty, tx), columns, columns],
        adjoint_init, land_mask, diffusivity, history, mixing, extract, coupling,
        hbm=tuple(range(7)),
        scratch=[
            pltpu.VMEM((nc, ty, tx), F32),
            pltpu.VMEM((ty, tx), jnp.int32),
            pltpu.VMEM(mixing.shape, F32),
            pltpu.VMEM(extract.shape, F32),
            pltpu.VMEM(coupling.shape, F32),
            pltpu.VMEM((-(-(steps + 1) * fields // SUB) * SUB, nc), F32),
            pltpu.SemaphoreType.DMA((6 + steps,)),
        ],
    )
    got = lax.ppermute(send, "sect", [(0, 1), (1, 0)])
    places, halo_count = field_places(steps, hf)
    blocks = -(-halo_count // per)
    total = 2 * (steps - 1) * fields + 2
    state_blocks = -(-total // per) + -(-nc // per)
    side = struct(ty, (blocks + state_blocks) * LANES)
    main, east, west = call(
        partial(force_kernel, places, halo_count, steps, fields),
        [struct(len(places), ty, tx), side, side],
        flag, keep, send, got, east, west,
        smem=(0,),
    )
    from_west, from_east = exchange(east, west, "gx", True)
    widths = with_packed(projected_widths(places, halo_count, steps), blocks, tx, hw)
    north, south = call(
        partial(rows_kernel, widths, blocks),
        [struct(strip_places(widths)[1], SUB, tx)] * 2,
        main, from_west, from_east,
    )
    from_north, from_south = exchange(south, north, "gy", False)
    dest = atmos_tile_index.reshape(tiles, entries)
    sel, weights = call(
        partial(select_kernel, cap, slots, nb),
        [struct(tiles * cap, slots), struct(cells, cells)],
        tile.reshape(1), dest, ocean_block_index.reshape(tiles, entries), regrid,
        smem=(0,),
    )
    [packed] = call(
        partial(surface_kernel, places, halo_count, widths, steps, hf),
        [struct(tiles * cap, steps * hf * LANES)],
        main, from_west, from_east, from_north, from_south, weights, sel,
        hbm_out=True,
        scratch=[pltpu.VMEM((tiles * cap, steps * hf * LANES), F32), pltpu.SemaphoreType.DMA((steps * hf,))],
    )
    widths = with_packed(state_widths(steps, fields, nc), state_blocks, tx, hw)
    sizes = (steps, fields, blocks, state_blocks)
    north, south = call(
        partial(state_rows_kernel, *sizes),
        [struct(strip_places(widths)[1], SUB, tx)] * 2,
        flag, adjoint_init, send, got, keep, from_west, from_east,
        smem=(0,),
        hbm=(1,),
        scratch=[pltpu.VMEM((2, nc, SUB, tx), F32), pltpu.SemaphoreType.DMA((2,))],
    )
    packed, dest, mixing, north, south = lax.optimization_barrier((packed, dest, mixing, north, south))
    arrived = lax.all_to_all(
        packed.reshape(tiles, cap, -1), ("gy", "gx"), split_axis=0, concat_axis=0, tiled=True
    ).reshape(tiles * cap, -1)

    from_north, from_south = exchange(south, north, "gy", False)
    terms = fields * steps * (steps + 1) // 2
    ext = (ty + SUB, tx + LANES)
    mix8, coup8, late = call(
        partial(matrices_kernel, steps, fields),
        [struct(nc * SUB, nc * SUB), struct(nc * SUB, 2 * fields * SUB), struct(nc * SUB, terms * SUB)],
        flag, mixing, coupling,
        smem=(0,),
    )
    base, ring = call(
        partial(state_kernel, *sizes),
        [struct(nc, ty, tx), struct(*ext)],
        flag, adjoint_init, send, got, keep, from_west, from_east, from_north, from_south, mix8, coup8,
        smem=(0,),
        hbm=(1,),
        scratch=[
            pltpu.VMEM((nc, *ext), F32),
            pltpu.VMEM((steps, 2 * fields, *ext), F32),
            pltpu.VMEM((nc, *ext), F32),
            pltpu.SemaphoreType.DMA,
        ],
    )

    [acc] = call(
        partial(arrival_kernel, cap, slots, nb),
        [struct(slots, tiles * cap)],
        tile.reshape(1), dest, atmos_block_index.reshape(tiles, entries),
        smem=(0,),
    )
    [own] = call(gather_kernel, [struct(steps * hf, ty, tx)], acc, arrived, ring)
    far = lax.ppermute(own, "sect", [(0, 1)])
    halo_count = (steps - 1) * fields
    blocks = -(-halo_count // per)
    east, west = call(partial(late_columns_kernel, steps), [struct(ty, blocks * LANES)] * 2, own, far)
    from_west, from_east = exchange(east, west, "gx", True, 1)
    widths = with_packed(late_widths(steps, fields), blocks, tx, hw)
    north, south = call(
        partial(late_rows_kernel, steps, blocks), [struct(strip_places(widths)[1], SUB, tx)] * 2, own, far, from_west, from_east
    )
    from_north, from_south = exchange(south, north, "gy", False, 1)
    [out] = call(
        partial(late_kernel, steps, blocks),
        [struct(1, nc, ty, tx)],
        flag, base, ring, late, own, far, from_west, from_east, from_north, from_south,
        smem=(0,),
        scratch=[pltpu.VMEM((terms, ty, tx), F32)],
    )
    return out


def solution(mesh):
    placed = (
        P("sect", None, "gy", "gx"),
        P("sect", "gy", "gx"),
        P("sect", None, None),
        P("sect", None, None),
        P("sect", None, None, "gy", "gx"),
        P(),
        P("gy", "gx"),
        P(("gy", "gx"), None, None),
        P(),
        P(),
        P(),
    )
    return jax.shard_map(
        body, mesh=mesh, in_specs=placed, out_specs=P("sect", None, "gy", "gx"), check_vma=False
    )
```

```python
import math

import jax
import jax.numpy as jnp
from jax import lax
from jax.experimental import pallas as pl
from jax.experimental.pallas import tpu as pltpu
from jax.sharding import PartitionSpec as P

LANES = 128
SUB = 8
F32 = jnp.float32
BF16 = jnp.bfloat16


LAST = (((1,), (1,)), ((), ()))


def full_dot(a, b, dims=(((1,), (0,)), ((), ()))):
    return lax.dot_general(a, b, dims, precision=lax.Precision.HIGHEST, preferred_element_type=F32)


def halves(x):
    high = x.astype(BF16)
    return high, (x - high.astype(F32)).astype(BF16)


def bf_dot(a, b, dims=(((1,), (0,)), ((), ()))):
    return lax.dot_general(a, b, dims, preferred_element_type=F32)


def dot3(a, b):
    (ah, al), (bh, bl) = a, b
    return bf_dot(ah, bh) + (bf_dot(ah, bl) + bf_dot(al, bh))


def grown(matrix):
    rows, cols = matrix.shape
    up = lax.broadcasted_iota(jnp.int32, (rows * SUB, rows), 0) // SUB
    up = (up == lax.broadcasted_iota(jnp.int32, (rows * SUB, rows), 1)).astype(F32)
    out = lax.broadcasted_iota(jnp.int32, (cols, cols * SUB), 1) // SUB
    out = (out == lax.broadcasted_iota(jnp.int32, (cols, cols * SUB), 0)).astype(F32)
    spread = full_dot(full_dot(up, matrix), out)
    i = lax.broadcasted_iota(jnp.int32, spread.shape, 0) % SUB
    j = lax.broadcasted_iota(jnp.int32, spread.shape, 1) % SUB
    return jnp.where(i == j, spread, 0.0)


def lane_ids(rows):
    return lax.broadcasted_iota(jnp.int32, (rows, LANES), 1)


def pack_columns(read, count, rows, tx, hw):
    per = LANES // hw
    ids = lane_ids(rows) // hw
    east, west = [], []
    last = tx // LANES - 1
    for block in range(-(-count // per)):
        e = jnp.zeros((rows, LANES), F32)
        w = jnp.zeros((rows, LANES), F32)
        for place in range(min(per, count - block * per)):
            f = block * per + place
            e_in, w_in = read(f, last), read(f, 0)
            e_shift, w_shift = (place * hw + hw) % LANES, place * hw
            e_in = pltpu.roll(e_in, e_shift, 1) if e_shift else e_in
            w_in = pltpu.roll(w_in, w_shift, 1) if w_shift else w_in
            e = jnp.where(ids == place, e_in, e)
            w = jnp.where(ids == place, w_in, w)
        east.append(e)
        west.append(w)
    return east, west


def store_columns(read, count, tx, hw, east_ref, west_ref, start):
    east, west = pack_columns(read, count, east_ref.shape[0], tx, hw)
    for block, (e, w) in enumerate(zip(east, west)):
        east_ref[:, (start + block) * LANES : (start + block + 1) * LANES] = e
        west_ref[:, (start + block) * LANES : (start + block + 1) * LANES] = w


def side_block(from_west, from_east, f, hw):
    place = f % (LANES // hw)
    ids = lane_ids(from_west.shape[0])
    e_shift, w_shift = (-place * hw) % LANES, (-hw - place * hw) % LANES
    e = pltpu.roll(from_east, e_shift, 1) if e_shift else from_east
    w = pltpu.roll(from_west, w_shift, 1) if w_shift else from_west
    return jnp.where(ids < hw, e, jnp.where(ids >= LANES - hw, w, 0.0))


def strip_places(widths):
    used, spots = [], [None] * len(widths)
    for f in sorted(range(len(widths)), key=lambda f: -widths[f]):
        t = next((t for t, rows in enumerate(used) if rows + widths[f] <= SUB), len(used))
        if t == len(used):
            used.append(0)
        spots[f] = (t, used[t])
        used[t] += widths[f]
    return spots, len(used)


def turn(x, by):
    return pltpu.roll(x, by % SUB, 0) if by % SUB else x


def edge_reader(north_ref, south_ref, widths):
    spots, _ = strip_places(widths)

    def edge(f, cols=slice(None)):
        (t, first), w = spots[f], widths[f]
        south = turn(south_ref[t, :, cols], -first)
        north = turn(north_ref[t, :, cols], -w - first)
        sub = lax.broadcasted_iota(jnp.int32, south.shape, 0)
        return jnp.where(sub < w, south, jnp.where(sub >= SUB - w, north, 0.0))

    return edge


def send_rows(read, widths, ty, north_ref, south_ref):
    spots, tiles = strip_places(widths)
    last = ty // SUB - 1
    sub = lax.broadcasted_iota(jnp.int32, north_ref.shape[1:], 0)
    for t in range(tiles):
        north = south = jnp.zeros(north_ref.shape[1:], F32)
        for f, (at, first) in enumerate(spots):
            if at == t:
                here = (sub >= first) & (sub < first + widths[f])
                north = jnp.where(here, turn(read(f, 0), first), north)
                south = jnp.where(here, turn(read(f, last), first + widths[f]), south)
        north_ref[t] = north
        south_ref[t] = south


def ring_lap(p):
    rows, cols = p.shape
    around = pltpu.roll(p, 1, 0) + pltpu.roll(p, rows - 1, 0)
    around = around + pltpu.roll(p, 1, 1) + pltpu.roll(p, cols - 1, 1)
    return around - 4.0 * p


def with_ring(main, packed_west, packed_east, f, edge, hw):
    bottom = edge(f)
    side = side_block(packed_west, packed_east, f, hw)
    return jnp.concatenate([jnp.concatenate([main, bottom], axis=0), side], axis=1)


def sides_with_rows(west_ref, east_ref, edge, first, start, blocks, tx):
    west, east = [], []
    per = tx // LANES
    for block in range(blocks):
        out = []
        for which, ref in enumerate((west_ref, east_ref)):
            f, at = divmod(which * blocks + block, per)
            tile = edge(first + f, slice(at * LANES, (at + 1) * LANES))
            out.append(jnp.concatenate([ref[:, pl.ds((start + block) * LANES, LANES)], tile], axis=0))
        west.append(out[0])
        east.append(out[1])
    return west, east


def packed_reader(west_ref, east_ref, start, blocks, tx):
    per = tx // LANES

    def read(f, row_tile):
        pieces = []
        for at in range(per):
            which, block = divmod(f * per + at, blocks)
            rows = pl.ds(row_tile * SUB, SUB)
            if which < 2:
                pieces.append((west_ref, east_ref)[which][rows, pl.ds((start + block) * LANES, LANES)])
            else:
                pieces.append(jnp.zeros((SUB, LANES), F32))
        return jnp.concatenate(pieces, axis=1)

    return read, -(-2 * blocks // per)


def with_packed(widths, blocks, tx, hw):
    return widths + [hw] * -(-2 * blocks * LANES // tx)


def projected_widths(places, halo_count, steps):
    widths = [0] * halo_count
    for key, f in places.items():
        if f < halo_count:
            widths[f] = steps if key == "d" else steps - 1 if key == "w" else steps - key[1] if key[0] == "t" else steps - 1 - key[1] - key[2]
    return widths


def state_widths(steps, fields, nc):
    return [k for _ in range(2) for k in range(1, steps) for _ in range(fields)] + [steps] * (2 + nc)


def late_widths(steps, fields):
    return [steps - 1 - n for n, _ in late_fields(steps, fields)]


def call(kernel, outs, *args, smem=(), hbm=(), hbm_out=False, scratch=(), flops=0):
    space = lambda i: pltpu.SMEM if i in smem else pltpu.HBM if i in hbm else pltpu.VMEM
    args = [pltpu.with_memory_space_constraint(a, pltpu.HBM) if i in hbm else a for i, a in enumerate(args)]
    nbytes = sum(math.prod(a.shape) * 4 for a in (*args, *outs))
    return pl.pallas_call(
        kernel,
        out_shape=[pltpu.HBM(o.shape, o.dtype) for o in outs] if hbm_out else outs,
        in_specs=[pl.BlockSpec(memory_space=space(i)) for i in range(len(args))],
        out_specs=[pl.BlockSpec(memory_space=pltpu.HBM if hbm_out else pltpu.VMEM) for _ in outs],
        scratch_shapes=scratch,
        compiler_params=pltpu.CompilerParams(vmem_limit_bytes=24 * 2**20),
        cost_estimate=pl.CostEstimate(flops=flops, bytes_accessed=nbytes, transcendentals=0),
    )(*args)


def stacked_rows(parts):
    high, low = halves(parts)
    return jnp.concatenate([high, high, low], axis=1)


def stacked_columns(parts):
    high, low = halves(parts)
    return jnp.concatenate([high, low, high], axis=0)


def project_kernel(
    adj_hbm, mask_hbm, diff_hbm, hist_hbm, mix_hbm, ext_hbm, coup_hbm,
    keep_ref, send_ref, east_ref, west_ref, adj_ref, mask_ref, mix_ref, ext_ref, coup_ref, chain_ref, sems,
):
    _, nc, ty, tx = adj_hbm.shape
    _, steps, fields = hist_hbm.shape[:3]
    hf = fields // 2
    count = (steps + 1) * hf
    copies = [
        pltpu.make_async_copy(mask_hbm, mask_ref, sems.at[0]),
        pltpu.make_async_copy(adj_hbm.at[0], adj_ref, sems.at[1]),
        pltpu.make_async_copy(diff_hbm.at[0], send_ref.at[count + 1], sems.at[2]),
    ]
    for k in range(steps):
        to = send_ref.at[pl.ds(count + 2 + k * fields, fields)]
        copies.append(pltpu.make_async_copy(hist_hbm.at[0, k], to, sems.at[3 + k]))
    small = [
        pltpu.make_async_copy(a, b, sems.at[3 + steps + i])
        for i, (a, b) in enumerate(((mix_hbm, mix_ref), (ext_hbm, ext_ref), (coup_hbm, coup_ref)))
    ]
    for copy in small + copies:
        copy.start()
    for copy in small:
        copy.wait()
    mix = mix_ref[0]
    rows = ext_ref[...]
    chain_ref[...] = jnp.zeros_like(chain_ref)
    for m in range(steps + 1):
        chain_ref[m * fields : (m + 1) * fields, :] = rows
        rows = rows + full_dot(rows, mix, LAST)
    chain = chain_ref[...]
    big = grown(chain)
    half = lambda x, h: jnp.concatenate(
        [x[(m * fields + h * hf) * SUB : (m * fields + (h + 1) * hf) * SUB] for m in range(steps + 1)], axis=0
    )
    force = grown(full_dot(chain, coup_ref[0], LAST))
    height, width = hf * SUB, force.shape[1]
    for m in range(steps):
        for h, ref in enumerate((keep_ref, send_ref)):
            per = ty // height
            r0, c0 = (m % per) * height, (m // per) * LANES
            at = (m * fields + h * hf) * SUB
            ref[count, r0 : r0 + height, c0 : c0 + width] = force[at : at + height]
    big = halves(jnp.concatenate([half(big, 0), half(big, 1)], axis=0))
    copies[0].wait()
    copies[1].wait()
    wet = mask_ref[...].astype(F32)
    keep_ref[count + 1] = wet
    for g in range(ty // SUB):
        rs = slice(g * SUB, (g + 1) * SUB)
        u = (adj_ref[:, rs, :] * wet[rs][None]).reshape(nc * SUB, tx)
        t = dot3(big, halves(u)).reshape(2 * count, SUB, tx)
        keep_ref[:count, rs, :] = t[:count]
        send_ref[:count, rs, :] = t[count:]
    store_columns(lambda f, l: adj_ref[f, :, l * LANES : (l + 1) * LANES], nc, tx, steps, east_ref, west_ref, 0)
    for copy in copies[2:]:
        copy.wait()


def field_places(steps, hf):
    with_halo, without = [], []
    for m in range(steps + 1):
        for q in range(hf):
            (with_halo if m < steps else without).append(("t", m, q))
    for n in range(steps):
        for m in range(steps - n):
            for q in range(hf):
                (with_halo if n + m < steps - 1 else without).append(("g", n, m, q))
    with_halo += ["d", "w"]
    return {key: i for i, key in enumerate(with_halo + without)}, len(with_halo)


def force_kernel(
    places, halo_count, steps, fields, flag_ref, keep_ref, send_ref, got_ref, adj_east_ref, adj_west_ref,
    sel_ref, main_ref, east_ref, west_ref,
):
    _, ty, tx = main_ref.shape
    hf, hw = fields // 2, steps
    count = (steps + 1) * hf
    ocean = flag_ref[0] == 0
    pick = lambda a, b: jnp.where(ocean, a, b)
    for m in range(steps + 1):
        for q in range(hf):
            main_ref[places["t", m, q]] = pick(keep_ref[m * hf + q], got_ref[m * hf + q])
    main_ref[places["d"]] = pick(send_ref[count + 1], got_ref[count + 1])
    main_ref[places["w"]] = keep_ref[count + 1]
    height, width = hf * SUB, 2 * fields * SUB
    per = ty // height
    big = []
    for m in range(steps):
        r0, c0 = (m % per) * height, (m // per) * LANES
        at = (count, slice(r0, r0 + height), slice(c0, c0 + width))
        big.append(pick(keep_ref[at], got_ref[at]))
    big = stacked_rows(jnp.concatenate(big, axis=0))
    for g in range(ty // SUB):
        rs = slice(g * SUB, (g + 1) * SUB)
        for n in range(steps):
            k = steps - 1 - n
            at = (slice(count + 2 + k * fields, count + 2 + (k + 1) * fields), rs)
            own, far = send_ref[at], got_ref[at]
            h = jnp.concatenate([pick(own, far), pick(far, own)], axis=0).reshape(-1, tx)
            out = bf_dot(big[: (steps - n) * height], stacked_columns(h))
            for m in range(steps - n):
                for q in range(hf):
                    at = (m * hf + q) * SUB
                    main_ref[places["g", n, m, q], rs, :] = out[at : at + SUB]
    read = lambda f, l: main_ref[f, :, l * LANES : (l + 1) * LANES]
    store_columns(read, halo_count, tx, hw, east_ref, west_ref, 0)
    start = -(-halo_count // (LANES // hw))
    state, total = forced_reader(steps, fields, flag_ref, send_ref, got_ref, keep_ref)
    read = lambda f, l: state(f, slice(0, ty), slice(l * LANES, (l + 1) * LANES))
    store_columns(read, total, tx, hw, east_ref, west_ref, start)
    start += -(-total // (LANES // hw))
    east_ref[:, start * LANES :] = adj_east_ref[...]
    west_ref[:, start * LANES :] = adj_west_ref[...]


def rows_kernel(widths, blocks, main_ref, west_ref, east_ref, north_ref, south_ref):
    _, ty, tx = main_ref.shape
    packed, more = packed_reader(west_ref, east_ref, 0, blocks, tx)
    count = len(widths) - more

    def read(f, t):
        return main_ref[f, t * SUB : (t + 1) * SUB, :] if f < count else packed(f - count, t)

    send_rows(read, widths, ty, north_ref, south_ref)


def block_place(slots, nb):
    return lambda b: (b % nb) * (slots // nb) + b // nb


def onehot(size, values):
    ids = lax.broadcasted_iota(jnp.int32, (size, values.shape[1]), 0)
    return (ids == values).astype(F32).astype(BF16)


def earlier(entries):
    row = lax.broadcasted_iota(jnp.int32, (entries, entries), 0)
    return row < lax.broadcasted_iota(jnp.int32, (entries, entries), 1)


def select_kernel(
    cap, slots, nb, pos_ref, dest_hbm, src_hbm, regrid_hbm, sel_ref, weights_ref, dest_ref, src_ref, sems
):
    tiles, entries = dest_ref.shape
    copies = [
        pltpu.make_async_copy(a, b, sems.at[i])
        for i, (a, b) in enumerate(((dest_hbm, dest_ref), (src_hbm, src_ref), (regrid_hbm.at[0], weights_ref)))
    ]
    for copy in copies:
        copy.start()
    for copy in copies:
        copy.wait()
    tile = pos_ref[0]
    dest = dest_ref[pl.ds(tile, 1), :]
    across = jnp.broadcast_to(dest.astype(F32), (entries, entries))
    same = (across == across.T) & earlier(entries)
    rank = jnp.sum(same.astype(F32), axis=0, keepdims=True).astype(jnp.int32)
    source = block_place(slots, nb)(src_ref[pl.ds(tile, 1), :])
    sel_ref[...] = bf_dot(onehot(tiles * cap, dest * cap + rank), onehot(slots, source), LAST)


def arrival_kernel(cap, slots, nb, pos_ref, dest_ref, dst_ref, acc_ref):
    tiles, entries = dest_ref.shape
    tile = pos_ref[0]
    acc_ref[...] = jnp.zeros_like(acc_ref)
    before = earlier(entries).astype(F32).astype(BF16)

    def source(i, carry):
        mine = dest_ref[pl.ds(i, 1), :] == tile
        mine_f = jnp.broadcast_to(mine.astype(F32), (SUB, entries)).astype(BF16)
        ranks = bf_dot(mine_f, before)[:1].astype(jnp.int32)
        spot = jnp.where(mine, i * cap + ranks, -1)
        place = block_place(slots, nb)(dst_ref[pl.ds(i, 1), :])
        acc_ref[...] += bf_dot(onehot(slots, place), onehot(tiles * cap, spot), LAST)
        return carry

    lax.fori_loop(0, tiles, source, 0, unroll=4)


def surface_kernel(
    places, halo_count, widths, steps, hf, main_ref, west_ref, east_ref, north_ref, south_ref, weights_ref, sel_ref,
    out_hbm, out_ref, sems,
):
    _, ty, tx = main_ref.shape
    hw = steps
    per = LANES // hw
    blocks = -(-halo_count // per)
    edge = edge_reader(north_ref, south_ref, widths)
    wests, easts = sides_with_rows(west_ref, east_ref, edge, halo_count, 0, blocks, tx)

    def ext(key):
        f = places[key]
        if f < halo_count:
            return with_ring(main_ref[f], wests[f // per], easts[f // per], f, edge, hw)
        main = jnp.concatenate([main_ref[f], jnp.zeros((SUB, tx), F32)], axis=0)
        return jnp.concatenate([main, jnp.zeros((ty + SUB, LANES), F32)], axis=1)

    diff, wet = ext("d"), ext("w")
    weights = halves(weights_ref[...])
    sel = sel_ref[...].astype(BF16)
    copies = []
    for q in range(hf):
        t = [ext(("t", m, q)) for m in range(steps + 1)]
        for n in range(steps):
            t = [wet * (t[m + 1] + ring_lap(diff * t[m]) + ext(("g", n, m, q))) for m in range(steps - n)]
            s = jnp.concatenate([t[0][:ty, l * LANES : (l + 1) * LANES] for l in range(tx // LANES)], axis=0)
            s = halves(dot3(halves(s), weights))
            at = (n * hf + q) * LANES
            out_ref[:, at : at + LANES] = bf_dot(sel, s[0]) + bf_dot(sel, s[1])
            to = out_hbm.at[:, pl.ds(at, LANES)]
            copies.append(pltpu.make_async_copy(out_ref.at[:, pl.ds(at, LANES)], to, sems.at[n * hf + q]))
            copies[-1].start()
    for copy in copies:
        copy.wait()


def gather_kernel(steps, flag_ref, acc_ref, in_ref, after_ref, out_ref, east_ref, west_ref):
    count, ty, tx = out_ref.shape
    hf = count // steps
    acc = acc_ref[...].astype(BF16)
    for i in range(count):
        high, low = halves(in_ref[:, i * LANES : (i + 1) * LANES])
        total = bf_dot(acc, high) + bf_dot(acc, low)
        for l in range(tx // LANES):
            out_ref[i, :, l * LANES : (l + 1) * LANES] = total[l * ty : (l + 1) * ty]
    todo = late_fields(steps, 2 * hf)

    def read(f, l):
        n, q = todo[f]
        return out_ref[n * hf + q, :, l * LANES : (l + 1) * LANES] if q < hf else jnp.zeros((ty, LANES), F32)

    store_columns(read, len(todo), tx, steps, east_ref, west_ref, 0)

    @pl.when(flag_ref[0] != 0)
    def _():
        for ref in (east_ref, west_ref):
            ref[...] = pltpu.roll(ref[...], hf * steps, 1)


def forced_reader(steps, fields, flag_ref, send_ref, got_ref, keep_ref):
    count = (steps + 1) * (fields // 2)
    forced = (steps - 1) * fields

    def read(f, rows, cols):
        if f < 2 * forced:
            part, f = divmod(f, forced)
            return (send_ref, got_ref)[part][count + 2 + fields + f, rows, cols]
        if f == 2 * forced:
            return send_ref[count + 1, rows, cols]
        return jnp.where(flag_ref[0] == 0, keep_ref[count + 1, rows, cols], 1.0)

    return read, 2 * forced + 2


def state_rows_kernel(
    steps, fields, start, blocks, flag_ref, adj_hbm, send_ref, got_ref, keep_ref, west_ref, east_ref,
    north_ref, south_ref, edges, sems,
):
    _, nc, ty, tx = adj_hbm.shape
    copies = [
        pltpu.make_async_copy(adj_hbm.at[0, :, pl.ds(t, SUB), :], edges.at[i], sems.at[i])
        for i, t in enumerate((0, ty - SUB))
    ]
    for copy in copies:
        copy.start()
    forced, total = forced_reader(steps, fields, flag_ref, send_ref, got_ref, keep_ref)
    packed, _ = packed_reader(west_ref, east_ref, start, blocks, tx)
    for copy in copies:
        copy.wait()

    def read(f, t):
        if f < total:
            return forced(f, slice(t * SUB, (t + 1) * SUB), slice(0, tx))
        f -= total
        return edges[min(t, 1), f] if f < nc else packed(f - nc, t)

    widths = with_packed(state_widths(steps, fields, nc), blocks, tx, steps)
    send_rows(read, widths, ty, north_ref, south_ref)


def matrices_kernel(steps, fields, flag_ref, mix_ref, coup_ref, mix8_ref, coup8_ref, late_ref):
    nc = mix_ref.shape[1]
    ident = lax.broadcasted_iota(jnp.int32, (nc, nc), 0) == lax.broadcasted_iota(jnp.int32, (nc, nc), 1)
    step_m = mix_ref[0].T + ident.astype(F32)
    coup = coup_ref[0].T
    late = coup[:, fields:]
    powers = []
    for i in range(steps):
        powers.append(late)
        late = full_dot(step_m, late)
    at = 0
    for k in range(steps - 1, -1, -1):
        for j in range(k + 1):
            late_ref[:, at : at + fields * SUB] = grown(math.comb(k, j) * powers[k - j])
            at += fields * SUB
    first = lax.broadcasted_iota(jnp.int32, coup.shape, 1) < fields
    mix8_ref[...] = grown(step_m)
    coup8_ref[...] = grown(jnp.where(jnp.logical_or(first, flag_ref[0] == 0), coup, 0.0))


def state_kernel(
    steps, fields, start, blocks, flag_ref, adj_hbm, send_ref, got_ref, keep_ref, west_ref, east_ref, north_ref,
    south_ref, mix8_ref, coup8_ref, out_ref, ring_ref, state, force, spread, sem,
):
    _, nc, ty, tx = adj_hbm.shape
    copy = pltpu.make_async_copy(adj_hbm.at[0], out_ref, sem)
    copy.start()
    hw = steps
    per = LANES // hw
    read, total = forced_reader(steps, fields, flag_ref, send_ref, got_ref, keep_ref)
    edge = edge_reader(north_ref, south_ref, with_packed(state_widths(steps, fields, nc), blocks, tx, hw))
    wests, easts = sides_with_rows(west_ref, east_ref, edge, total + nc, start, blocks, tx)

    def ext(f):
        main = read(f, slice(0, ty), slice(0, tx))
        return with_ring(main, wests[f // per], easts[f // per], f, edge, hw)

    forced = (steps - 1) * fields
    for k in range(1, steps):
        for q in range(fields):
            force[k, q] = ext((k - 1) * fields + q)
            force[k, fields + q] = ext(forced + (k - 1) * fields + q)
    at = (steps + 1) * (fields // 2) + 2
    for q in range(fields):
        force[0, q, :ty, :tx] = send_ref[at + q]
        force[0, fields + q, :ty, :tx] = got_ref[at + q]
    diff, wet = ext(2 * forced), ext(2 * forced + 1)
    ring_ref[...] = diff
    mix8, coup8 = halves(mix8_ref[...]), stacked_rows(coup8_ref[...])
    groups = ty // SUB
    main = [((g, 0, tx),) for g in range(groups)]
    halo = [((groups, 0, tx),)] + [
        tuple((g, tx, LANES) for g in range(at, min(at + tx // LANES, groups + 1)))
        for at in range(0, groups + 1, tx // LANES)
    ]
    copy.wait()
    block = -(-total // per)
    for c in range(nc):
        west, east = wests[block + c // per], easts[block + c // per]
        state[c, :ty, :tx] = out_ref[c]
        state[c, ty:, :tx] = edge(total + c)
        state[c, :, tx:] = side_block(west, east, c, hw)

    for n in range(steps):
        k = steps - 1 - n
        small = n == steps - 1

        def one(c, carry):
            u = wet * state[c]
            state[c] = u
            spread[c] = ring_lap(diff * u)
            return carry

        lax.fori_loop(0, nc, one, 0, unroll=True)
        for places in main if small else main + halo:
            spots = [(slice(g * SUB, (g + 1) * SUB), slice(c, c + w)) for g, c, w in places]
            u = jnp.concatenate([state[:, rs, cs].reshape(nc * SUB, -1) for rs, cs in spots], axis=1)
            h = jnp.concatenate([force[k, :, rs, cs].reshape(2 * fields * SUB, -1) for rs, cs in spots], axis=1)
            new = dot3(mix8, halves(u)) + bf_dot(coup8, stacked_columns(h))
            at = 0
            for (rs, cs), (_, _, w) in zip(spots, places):
                value = new[:, at : at + w].reshape(nc, SUB, w) + spread[:, rs, cs]
                at += w
                if small:
                    out_ref[:, rs, cs] = value
                else:
                    state[:, rs, cs] = value


def late_fields(steps, fields):
    return [(n, q) for n in range(steps - 1) for q in range(fields)]


def late_main(steps, hf, own_ref, far_ref):
    def read(n, q):
        return far_ref[n * hf + q] if q < hf else own_ref[n * hf + q - hf]

    return read


def late_rows_kernel(
    steps, blocks, own_ref, far_ref, west0_ref, west1_ref, east0_ref, east1_ref, north_ref, south_ref, west_ref, east_ref
):
    west_ref[...] = west0_ref[...] + west1_ref[...]
    east_ref[...] = east0_ref[...] + east1_ref[...]
    count, ty, tx = own_ref.shape
    hf = count // steps
    todo = late_fields(steps, 2 * hf)
    packed, _ = packed_reader(west_ref, east_ref, 0, blocks, tx)

    def read(f, t):
        if f >= len(todo):
            return packed(f - len(todo), t)
        n, q = todo[f]
        ref, i = (far_ref, n * hf + q) if q < hf else (own_ref, n * hf + q - hf)
        return ref[i, t * SUB : (t + 1) * SUB, :]

    send_rows(read, with_packed(late_widths(steps, 2 * hf), blocks, tx, steps), ty, north_ref, south_ref)


def late_kernel(
    steps, blocks, flag_ref, base_ref, ring_ref, late_ref, own_ref, far_ref, west_ref, east_ref, north_ref, south_ref,
    out_ref, stack,
):
    count, ty, tx = own_ref.shape
    hf = count // steps
    fields = 2 * hf
    nc = base_ref.shape[0]
    per = LANES // steps
    todo = late_fields(steps, fields)
    read = late_main(steps, hf, own_ref, far_ref)

    @pl.when(flag_ref[0] == 0)
    def _():
        out_ref[0] = base_ref[...]

    @pl.when(flag_ref[0] != 0)
    def _():
        diff = ring_ref[...]
        edge = edge_reader(north_ref, south_ref, with_packed(late_widths(steps, fields), blocks, tx, steps))
        wests, easts = sides_with_rows(west_ref, east_ref, edge, len(todo), 0, blocks, tx)
        at = 0
        for n in range(steps):
            k = steps - 1 - n
            for q in range(fields):
                r = read(n, q)
                if k:
                    f = todo.index((n, q))
                    r = with_ring(r, wests[f // per], easts[f // per], f, edge, steps)
                for j in range(k + 1):
                    stack[at + j * fields + q] = r[:ty, :tx]
                    if j < k:
                        r = ring_lap(diff * r)
            at += (k + 1) * fields
        big = halves(late_ref[...])
        for g in range(ty // SUB):
            rs = slice(g * SUB, (g + 1) * SUB)
            more = dot3(big, halves(stack[:, rs, :].reshape(-1, tx)))
            out_ref[0, :, rs, :] = base_ref[:, rs, :] + more.reshape(nc, SUB, tx)


def shifted(x, axis, by, wrap, sects=None):
    size = lax.axis_size(axis)
    pairs = [(i, (i + by) % size) for i in range(size) if wrap or 0 <= i + by < size]
    if sects is None:
        return lax.ppermute(x, axis, pairs)
    a, b = sects
    return lax.ppermute(x, ("sect", axis), [(a * size + i, b * size + j) for i, j in pairs])


def struct(*shape):
    return jax.ShapeDtypeStruct(shape, F32)


def partial(kernel, *args):
    def run(*refs):
        kernel(*args, *refs)

    run.__name__ = kernel.__name__
    return run


def body(
    adjoint_init,
    diffusivity,
    mixing,
    coupling,
    history,
    extract,
    land_mask,
    regrid,
    atmos_tile_index,
    ocean_block_index,
    atmos_block_index,
):
    _, steps, fields, ty, tx = history.shape
    nc = adjoint_init.shape[1]
    hf, hw = fields // 2, steps
    per = LANES // hw
    sect = lax.axis_index("sect").astype(jnp.int32)
    tile = (lax.axis_index("gy") * lax.axis_size("gx") + lax.axis_index("gx")).astype(jnp.int32)
    flag = sect.reshape(1)
    tiles = lax.axis_size("gy") * lax.axis_size("gx")
    entries = ocean_block_index.shape[0] // tiles
    cap = 2 * entries // tiles
    cells = regrid.shape[1]
    slots = ty * tx // cells
    nb = tx // cells

    def exchange(x_after, x_before, axis, wrap, only=None):
        return shifted(x_after, axis, 1, wrap, only), shifted(x_before, axis, -1, wrap, only)

    count = (steps + 1) * hf
    coupling = jnp.swapaxes(coupling, 1, 2)
    columns = struct(ty, -(-nc // per) * LANES)
    keep, send, east, west = call(
        project_kernel,
        [struct(count + 2, ty, tx), struct(count + 2 + steps * fields, ty, tx), columns, columns],
        adjoint_init, land_mask, diffusivity, history, mixing, extract, coupling,
        hbm=tuple(range(7)),
        scratch=[
            pltpu.VMEM((nc, ty, tx), F32),
            pltpu.VMEM((ty, tx), jnp.int32),
            pltpu.VMEM(mixing.shape, F32),
            pltpu.VMEM(extract.shape, F32),
            pltpu.VMEM(coupling.shape, F32),
            pltpu.VMEM((-(-(steps + 1) * fields // SUB) * SUB, nc), F32),
            pltpu.SemaphoreType.DMA((6 + steps,)),
        ],
    )
    got = lax.ppermute(send, "sect", [(0, 1), (1, 0)])
    dest = atmos_tile_index.reshape(tiles, entries)
    sel, weights = call(
        partial(select_kernel, cap, slots, nb),
        [struct(tiles * cap, slots), struct(cells, cells)],
        tile.reshape(1), dest, ocean_block_index.reshape(tiles, entries), regrid,
        smem=(0,),
        hbm=(1, 2, 3),
        scratch=[pltpu.VMEM((tiles, entries), jnp.int32)] * 2 + [pltpu.SemaphoreType.DMA((3,))],
    )
    places, halo_count = field_places(steps, hf)
    blocks = -(-halo_count // per)
    total = 2 * (steps - 1) * fields + 2
    state_blocks = -(-total // per) + -(-nc // per)
    side = struct(ty, (blocks + state_blocks) * LANES)
    main, east, west = call(
        partial(force_kernel, places, halo_count, steps, fields),
        [struct(len(places), ty, tx), side, side],
        flag, keep, send, got, east, west, sel,
        smem=(0,),
    )
    from_west, from_east = exchange(east, west, "gx", True)
    widths = with_packed(projected_widths(places, halo_count, steps), blocks, tx, hw)
    north, south = call(
        partial(rows_kernel, widths, blocks),
        [struct(strip_places(widths)[1], SUB, tx)] * 2,
        main, from_west, from_east,
    )
    from_north, from_south = exchange(south, north, "gy", False)
    [packed] = call(
        partial(surface_kernel, places, halo_count, widths, steps, hf),
        [struct(tiles * cap, steps * hf * LANES)],
        main, from_west, from_east, from_north, from_south, weights, sel,
        hbm_out=True,
        scratch=[pltpu.VMEM((tiles * cap, steps * hf * LANES), F32), pltpu.SemaphoreType.DMA((steps * hf,))],
    )
    widths = with_packed(state_widths(steps, fields, nc), state_blocks, tx, hw)
    sizes = (steps, fields, blocks, state_blocks)
    north, south = call(
        partial(state_rows_kernel, *sizes),
        [struct(strip_places(widths)[1], SUB, tx)] * 2,
        flag, adjoint_init, send, got, keep, from_west, from_east,
        smem=(0,),
        hbm=(1,),
        scratch=[pltpu.VMEM((2, nc, SUB, tx), F32), pltpu.SemaphoreType.DMA((2,))],
    )
    packed, dest, mixing, north, south = lax.optimization_barrier((packed, dest, mixing, north, south))
    arrived = lax.all_to_all(
        packed.reshape(tiles, cap, -1), ("gy", "gx"), split_axis=0, concat_axis=0, tiled=True
    ).reshape(tiles * cap, -1)

    from_north, from_south = exchange(south, north, "gy", False)
    terms = fields * steps * (steps + 1) // 2
    ext = (ty + SUB, tx + LANES)
    mix8, coup8, late = call(
        partial(matrices_kernel, steps, fields),
        [struct(nc * SUB, nc * SUB), struct(nc * SUB, 2 * fields * SUB), struct(nc * SUB, terms * SUB)],
        flag, mixing, coupling,
        smem=(0,),
    )
    base, ring = call(
        partial(state_kernel, *sizes),
        [struct(nc, ty, tx), struct(*ext)],
        flag, adjoint_init, send, got, keep, from_west, from_east, from_north, from_south, mix8, coup8,
        smem=(0,),
        hbm=(1,),
        scratch=[
            pltpu.VMEM((nc, *ext), F32),
            pltpu.VMEM((steps, 2 * fields, *ext), F32),
            pltpu.VMEM((nc, *ext), F32),
            pltpu.SemaphoreType.DMA,
        ],
    )

    [acc] = call(
        partial(arrival_kernel, cap, slots, nb),
        [struct(slots, tiles * cap)],
        tile.reshape(1), dest, atmos_block_index.reshape(tiles, entries),
        smem=(0,),
    )
    halo_count = (steps - 1) * fields
    blocks = -(-halo_count // per)
    side = struct(ty, blocks * LANES)
    own, east, west = call(
        partial(gather_kernel, steps), [struct(steps * hf, ty, tx), side, side], flag, acc, arrived, ring, smem=(0,)
    )
    far = lax.ppermute(own, "sect", [(0, 1)])
    west1, east1 = exchange(east, west, "gx", True, (1, 1))
    west0, east0 = exchange(east, west, "gx", True, (0, 1))
    widths = with_packed(late_widths(steps, fields), blocks, tx, hw)
    rows = struct(strip_places(widths)[1], SUB, tx)
    north, south, from_west, from_east = call(
        partial(late_rows_kernel, steps, blocks), [rows, rows, side, side], own, far, west0, west1, east0, east1
    )
    from_north, from_south = exchange(south, north, "gy", False, (1, 1))
    [out] = call(
        partial(late_kernel, steps, blocks),
        [struct(1, nc, ty, tx)],
        flag, base, ring, late, own, far, from_west, from_east, from_north, from_south,
        smem=(0,),
        scratch=[pltpu.VMEM((terms, ty, tx), F32)],
    )
    return out


def solution(mesh):
    placed = (
        P("sect", None, "gy", "gx"),
        P("sect", "gy", "gx"),
        P("sect", None, None),
        P("sect", None, None),
        P("sect", None, None, "gy", "gx"),
        P(),
        P("gy", "gx"),
        P(("gy", "gx"), None, None),
        P(),
        P(),
        P(),
    )
    return jax.shard_map(
        body, mesh=mesh, in_specs=placed, out_specs=P("sect", None, "gy", "gx"), check_vma=False
    )
```

```python
import math

import jax
import jax.numpy as jnp
from jax import lax
from jax.experimental import pallas as pl
from jax.experimental.pallas import tpu as pltpu
from jax.sharding import PartitionSpec as P

LANES = 128
SUB = 8
F32 = jnp.float32
BF16 = jnp.bfloat16


LAST = (((1,), (1,)), ((), ()))


def full_dot(a, b, dims=(((1,), (0,)), ((), ()))):
    return lax.dot_general(a, b, dims, precision=lax.Precision.HIGHEST, preferred_element_type=F32)


def halves(x):
    high = x.astype(BF16)
    return high, (x - high.astype(F32)).astype(BF16)


def bf_dot(a, b, dims=(((1,), (0,)), ((), ()))):
    return lax.dot_general(a, b, dims, preferred_element_type=F32)


def dot3(a, b):
    (ah, al), (bh, bl) = a, b
    return bf_dot(ah, bh) + (bf_dot(ah, bl) + bf_dot(al, bh))


def grown(matrix):
    rows, cols = matrix.shape
    up = lax.broadcasted_iota(jnp.int32, (rows * SUB, rows), 0) // SUB
    up = (up == lax.broadcasted_iota(jnp.int32, (rows * SUB, rows), 1)).astype(F32)
    out = lax.broadcasted_iota(jnp.int32, (cols, cols * SUB), 1) // SUB
    out = (out == lax.broadcasted_iota(jnp.int32, (cols, cols * SUB), 0)).astype(F32)
    spread = full_dot(full_dot(up, matrix), out)
    i = lax.broadcasted_iota(jnp.int32, spread.shape, 0) % SUB
    j = lax.broadcasted_iota(jnp.int32, spread.shape, 1) % SUB
    return jnp.where(i == j, spread, 0.0)


def lane_ids(rows):
    return lax.broadcasted_iota(jnp.int32, (rows, LANES), 1)


def pack_columns(read, count, rows, tx, hw):
    per = LANES // hw
    ids = lane_ids(rows) // hw
    east, west = [], []
    last = tx // LANES - 1
    for block in range(-(-count // per)):
        e = jnp.zeros((rows, LANES), F32)
        w = jnp.zeros((rows, LANES), F32)
        for place in range(min(per, count - block * per)):
            f = block * per + place
            e_in, w_in = read(f, last), read(f, 0)
            e_shift, w_shift = (place * hw + hw) % LANES, place * hw
            e_in = pltpu.roll(e_in, e_shift, 1) if e_shift else e_in
            w_in = pltpu.roll(w_in, w_shift, 1) if w_shift else w_in
            e = jnp.where(ids == place, e_in, e)
            w = jnp.where(ids == place, w_in, w)
        east.append(e)
        west.append(w)
    return east, west


def store_columns(read, count, tx, hw, east_ref, west_ref, start):
    east, west = pack_columns(read, count, east_ref.shape[0], tx, hw)
    for block, (e, w) in enumerate(zip(east, west)):
        east_ref[:, (start + block) * LANES : (start + block + 1) * LANES] = e
        west_ref[:, (start + block) * LANES : (start + block + 1) * LANES] = w


def side_block(from_west, from_east, f, hw):
    place = f % (LANES // hw)
    ids = lane_ids(from_west.shape[0])
    e_shift, w_shift = (-place * hw) % LANES, (-hw - place * hw) % LANES
    e = pltpu.roll(from_east, e_shift, 1) if e_shift else from_east
    w = pltpu.roll(from_west, w_shift, 1) if w_shift else from_west
    return jnp.where(ids < hw, e, jnp.where(ids >= LANES - hw, w, 0.0))


def strip_places(widths):
    used, spots = [], [None] * len(widths)
    for f in sorted(range(len(widths)), key=lambda f: -widths[f]):
        t = next((t for t, rows in enumerate(used) if rows + widths[f] <= SUB), len(used))
        if t == len(used):
            used.append(0)
        spots[f] = (t, used[t])
        used[t] += widths[f]
    return spots, len(used)


def turn(x, by):
    return pltpu.roll(x, by % SUB, 0) if by % SUB else x


def edge_reader(north_ref, south_ref, widths):
    spots, _ = strip_places(widths)

    def edge(f, cols=slice(None)):
        (t, first), w = spots[f], widths[f]
        south = turn(south_ref[t, :, cols], -first)
        north = turn(north_ref[t, :, cols], -w - first)
        sub = lax.broadcasted_iota(jnp.int32, south.shape, 0)
        return jnp.where(sub < w, south, jnp.where(sub >= SUB - w, north, 0.0))

    return edge


def send_rows(read, widths, ty, north_ref, south_ref):
    spots, tiles = strip_places(widths)
    last = ty // SUB - 1
    sub = lax.broadcasted_iota(jnp.int32, north_ref.shape[1:], 0)
    for t in range(tiles):
        north = south = jnp.zeros(north_ref.shape[1:], F32)
        for f, (at, first) in enumerate(spots):
            if at == t:
                here = (sub >= first) & (sub < first + widths[f])
                north = jnp.where(here, turn(read(f, 0), first), north)
                south = jnp.where(here, turn(read(f, last), first + widths[f]), south)
        north_ref[t] = north
        south_ref[t] = south


def ring_lap(p):
    rows, cols = p.shape
    around = pltpu.roll(p, 1, 0) + pltpu.roll(p, rows - 1, 0)
    around = around + pltpu.roll(p, 1, 1) + pltpu.roll(p, cols - 1, 1)
    return around - 4.0 * p


def with_ring(main, packed_west, packed_east, f, edge, hw):
    bottom = edge(f)
    side = side_block(packed_west, packed_east, f, hw)
    return jnp.concatenate([jnp.concatenate([main, bottom], axis=0), side], axis=1)


def sides_with_rows(west_ref, east_ref, edge, first, start, blocks, tx):
    west, east = [], []
    per = tx // LANES
    for block in range(blocks):
        out = []
        for which, ref in enumerate((west_ref, east_ref)):
            f, at = divmod(which * blocks + block, per)
            tile = edge(first + f, slice(at * LANES, (at + 1) * LANES))
            out.append(jnp.concatenate([ref[:, pl.ds((start + block) * LANES, LANES)], tile], axis=0))
        west.append(out[0])
        east.append(out[1])
    return west, east


def packed_reader(west_ref, east_ref, start, blocks, tx):
    per = tx // LANES

    def read(f, row_tile):
        pieces = []
        for at in range(per):
            which, block = divmod(f * per + at, blocks)
            rows = pl.ds(row_tile * SUB, SUB)
            if which < 2:
                pieces.append((west_ref, east_ref)[which][rows, pl.ds((start + block) * LANES, LANES)])
            else:
                pieces.append(jnp.zeros((SUB, LANES), F32))
        return jnp.concatenate(pieces, axis=1)

    return read, -(-2 * blocks // per)


def with_packed(widths, blocks, tx, hw):
    return widths + [hw] * -(-2 * blocks * LANES // tx)


def projected_widths(places, halo_count, steps):
    widths = [0] * halo_count
    for key, f in places.items():
        if f < halo_count:
            widths[f] = steps if key == "d" else steps - 1 if key == "w" else steps - key[1] if key[0] == "t" else steps - 1 - key[1] - key[2]
    return widths


def state_widths(steps, fields, nc):
    return [k for _ in range(2) for k in range(1, steps) for _ in range(fields)] + [steps] * (2 + nc)


def late_widths(steps, fields):
    return [steps - 1 - n for n, _ in late_fields(steps, fields)]


def call(kernel, outs, *args, smem=(), hbm=(), hbm_out=(), scratch=(), flops=0):
    space = lambda i: pltpu.SMEM if i in smem else pltpu.HBM if i in hbm else pltpu.VMEM
    args = [pltpu.with_memory_space_constraint(a, pltpu.HBM) if i in hbm else a for i, a in enumerate(args)]
    nbytes = sum(math.prod(a.shape) * 4 for a in (*args, *outs))
    return pl.pallas_call(
        kernel,
        out_shape=[pltpu.HBM(o.shape, o.dtype) if i in hbm_out else o for i, o in enumerate(outs)],
        in_specs=[pl.BlockSpec(memory_space=space(i)) for i in range(len(args))],
        out_specs=[pl.BlockSpec(memory_space=pltpu.HBM if i in hbm_out else pltpu.VMEM) for i in range(len(outs))],
        scratch_shapes=scratch,
        compiler_params=pltpu.CompilerParams(vmem_limit_bytes=24 * 2**20),
        cost_estimate=pl.CostEstimate(flops=flops, bytes_accessed=nbytes, transcendentals=0),
    )(*args)


def stacked_rows(parts):
    high, low = halves(parts)
    return jnp.concatenate([high, high, low], axis=1)


def stacked_columns(parts):
    high, low = halves(parts)
    return jnp.concatenate([high, low, high], axis=0)


def project_kernel(
    adj_hbm, mask_hbm, diff_hbm, hist_hbm, mix_hbm, ext_hbm, coup_hbm,
    keep_ref, send_ref, east_ref, west_ref, adj_ref, mask_ref, mix_ref, ext_ref, coup_ref, chain_ref, sems,
):
    _, nc, ty, tx = adj_hbm.shape
    _, steps, fields = hist_hbm.shape[:3]
    hf = fields // 2
    count = (steps + 1) * hf
    copies = [
        pltpu.make_async_copy(mask_hbm, mask_ref, sems.at[0]),
        pltpu.make_async_copy(adj_hbm.at[0], adj_ref, sems.at[1]),
        pltpu.make_async_copy(diff_hbm.at[0], send_ref.at[count + 1], sems.at[2]),
    ]
    for k in range(steps):
        to = send_ref.at[pl.ds(count + 2 + k * fields, fields)]
        copies.append(pltpu.make_async_copy(hist_hbm.at[0, k], to, sems.at[3 + k]))
    small = [
        pltpu.make_async_copy(a, b, sems.at[3 + steps + i])
        for i, (a, b) in enumerate(((mix_hbm, mix_ref), (ext_hbm, ext_ref), (coup_hbm, coup_ref)))
    ]
    for copy in small + copies:
        copy.start()
    for copy in small:
        copy.wait()
    mix = mix_ref[0]
    rows = ext_ref[...]
    chain_ref[...] = jnp.zeros_like(chain_ref)
    for m in range(steps + 1):
        chain_ref[m * fields : (m + 1) * fields, :] = rows
        rows = rows + full_dot(rows, mix, LAST)
    chain = chain_ref[...]
    big = grown(chain)
    half = lambda x, h: jnp.concatenate(
        [x[(m * fields + h * hf) * SUB : (m * fields + (h + 1) * hf) * SUB] for m in range(steps + 1)], axis=0
    )
    force = grown(full_dot(chain, coup_ref[0], LAST))
    height, width = hf * SUB, force.shape[1]
    for m in range(steps):
        for h, ref in enumerate((keep_ref, send_ref)):
            per = ty // height
            r0, c0 = (m % per) * height, (m // per) * LANES
            at = (m * fields + h * hf) * SUB
            ref[count, r0 : r0 + height, c0 : c0 + width] = force[at : at + height]
    big = halves(jnp.concatenate([half(big, 0), half(big, 1)], axis=0))
    copies[0].wait()
    copies[1].wait()
    wet = mask_ref[...].astype(F32)
    keep_ref[count + 1] = wet
    for g in range(ty // SUB):
        rs = slice(g * SUB, (g + 1) * SUB)
        u = (adj_ref[:, rs, :] * wet[rs][None]).reshape(nc * SUB, tx)
        t = dot3(big, halves(u)).reshape(2 * count, SUB, tx)
        keep_ref[:count, rs, :] = t[:count]
        send_ref[:count, rs, :] = t[count:]
    store_columns(lambda f, l: adj_ref[f, :, l * LANES : (l + 1) * LANES], nc, tx, steps, east_ref, west_ref, 0)
    for copy in copies[2:]:
        copy.wait()


def field_places(steps, hf):
    with_halo, without = [], []
    for m in range(steps + 1):
        for q in range(hf):
            (with_halo if m < steps else without).append(("t", m, q))
    for n in range(steps):
        for m in range(steps - n):
            for q in range(hf):
                (with_halo if n + m < steps - 1 else without).append(("g", n, m, q))
    with_halo += ["d", "w"]
    return {key: i for i, key in enumerate(with_halo + without)}, len(with_halo)


def force_kernel(
    places, halo_count, steps, fields, flag_ref, keep_ref, send_ref, got_ref, adj_east_ref, adj_west_ref,
    sel_ref, main_ref, east_ref, west_ref,
):
    _, ty, tx = main_ref.shape
    hf, hw = fields // 2, steps
    count = (steps + 1) * hf
    ocean = flag_ref[0] == 0
    pick = lambda a, b: jnp.where(ocean, a, b)
    for m in range(steps + 1):
        for q in range(hf):
            main_ref[places["t", m, q]] = pick(keep_ref[m * hf + q], got_ref[m * hf + q])
    main_ref[places["d"]] = pick(send_ref[count + 1], got_ref[count + 1])
    main_ref[places["w"]] = keep_ref[count + 1]
    height, width = hf * SUB, 2 * fields * SUB
    per = ty // height
    big = []
    for m in range(steps):
        r0, c0 = (m % per) * height, (m // per) * LANES
        at = (count, slice(r0, r0 + height), slice(c0, c0 + width))
        big.append(pick(keep_ref[at], got_ref[at]))
    big = stacked_rows(jnp.concatenate(big, axis=0))
    for g in range(ty // SUB):
        rs = slice(g * SUB, (g + 1) * SUB)
        for n in range(steps):
            k = steps - 1 - n
            at = (slice(count + 2 + k * fields, count + 2 + (k + 1) * fields), rs)
            own, far = send_ref[at], got_ref[at]
            h = jnp.concatenate([pick(own, far), pick(far, own)], axis=0).reshape(-1, tx)
            out = bf_dot(big[: (steps - n) * height], stacked_columns(h))
            for m in range(steps - n):
                for q in range(hf):
                    at = (m * hf + q) * SUB
                    main_ref[places["g", n, m, q], rs, :] = out[at : at + SUB]
    read = lambda f, l: main_ref[f, :, l * LANES : (l + 1) * LANES]
    store_columns(read, halo_count, tx, hw, east_ref, west_ref, 0)
    start = -(-halo_count // (LANES // hw))
    state, total = forced_reader(steps, fields, flag_ref, send_ref, got_ref, keep_ref)
    read = lambda f, l: state(f, slice(0, ty), slice(l * LANES, (l + 1) * LANES))
    store_columns(read, total, tx, hw, east_ref, west_ref, start)
    start += -(-total // (LANES // hw))
    east_ref[:, start * LANES :] = adj_east_ref[...]
    west_ref[:, start * LANES :] = adj_west_ref[...]


def rows_kernel(widths, blocks, main_ref, west_ref, east_ref, north_ref, south_ref):
    _, ty, tx = main_ref.shape
    packed, more = packed_reader(west_ref, east_ref, 0, blocks, tx)
    count = len(widths) - more

    def read(f, t):
        return main_ref[f, t * SUB : (t + 1) * SUB, :] if f < count else packed(f - count, t)

    send_rows(read, widths, ty, north_ref, south_ref)


def block_place(slots, nb):
    return lambda b: (b % nb) * (slots // nb) + b // nb


def onehot(size, values):
    ids = lax.broadcasted_iota(jnp.int32, (size, values.shape[1]), 0)
    return (ids == values).astype(F32).astype(BF16)


def earlier(entries):
    row = lax.broadcasted_iota(jnp.int32, (entries, entries), 0)
    return row < lax.broadcasted_iota(jnp.int32, (entries, entries), 1)


def select_kernel(
    cap, slots, nb, pos_ref, dest_hbm, src_hbm, regrid_hbm, sel_ref, weights_ref, dest_ref, src_ref, sems
):
    tiles, entries = dest_ref.shape
    copies = [
        pltpu.make_async_copy(a, b, sems.at[i])
        for i, (a, b) in enumerate(((dest_hbm, dest_ref), (src_hbm, src_ref), (regrid_hbm.at[0], weights_ref)))
    ]
    for copy in copies:
        copy.start()
    for copy in copies:
        copy.wait()
    tile = pos_ref[0]
    dest = dest_ref[pl.ds(tile, 1), :]
    across = jnp.broadcast_to(dest.astype(F32), (entries, entries))
    same = (across == across.T) & earlier(entries)
    rank = jnp.sum(same.astype(F32), axis=0, keepdims=True).astype(jnp.int32)
    source = block_place(slots, nb)(src_ref[pl.ds(tile, 1), :])
    sel_ref[...] = bf_dot(onehot(tiles * cap, dest * cap + rank), onehot(slots, source), LAST)


def arrival_kernel(cap, slots, nb, pos_ref, dest_ref, dst_ref, acc_ref):
    tiles, entries = dest_ref.shape
    tile = pos_ref[0]
    acc_ref[...] = jnp.zeros_like(acc_ref)
    before = earlier(entries).astype(F32).astype(BF16)

    def source(i, carry):
        mine = dest_ref[pl.ds(i, 1), :] == tile
        mine_f = jnp.broadcast_to(mine.astype(F32), (SUB, entries)).astype(BF16)
        ranks = bf_dot(mine_f, before)[:1].astype(jnp.int32)
        spot = jnp.where(mine, i * cap + ranks, -1)
        place = block_place(slots, nb)(dst_ref[pl.ds(i, 1), :])
        acc_ref[...] += bf_dot(onehot(slots, place), onehot(tiles * cap, spot), LAST)
        return carry

    lax.fori_loop(0, tiles, source, 0, unroll=4)


def surface_kernel(
    places, halo_count, widths, steps, hf, main_ref, west_ref, east_ref, north_ref, south_ref, weights_ref, sel_ref,
    out_hbm, out_ref, sems,
):
    _, ty, tx = main_ref.shape
    hw = steps
    per = LANES // hw
    blocks = -(-halo_count // per)
    edge = edge_reader(north_ref, south_ref, widths)
    wests, easts = sides_with_rows(west_ref, east_ref, edge, halo_count, 0, blocks, tx)

    def ext(key):
        f = places[key]
        if f < halo_count:
            return with_ring(main_ref[f], wests[f // per], easts[f // per], f, edge, hw)
        main = jnp.concatenate([main_ref[f], jnp.zeros((SUB, tx), F32)], axis=0)
        return jnp.concatenate([main, jnp.zeros((ty + SUB, LANES), F32)], axis=1)

    diff, wet = ext("d"), ext("w")
    weights = halves(weights_ref[...])
    sel = sel_ref[...].astype(BF16)
    copies = []
    for q in range(hf):
        t = [ext(("t", m, q)) for m in range(steps + 1)]
        for n in range(steps):
            t = [wet * (t[m + 1] + ring_lap(diff * t[m]) + ext(("g", n, m, q))) for m in range(steps - n)]
            s = jnp.concatenate([t[0][:ty, l * LANES : (l + 1) * LANES] for l in range(tx // LANES)], axis=0)
            s = halves(dot3(halves(s), weights))
            at = (n * hf + q) * LANES
            out_ref[:, at : at + LANES] = bf_dot(sel, s[0]) + bf_dot(sel, s[1])
            to = out_hbm.at[:, pl.ds(at, LANES)]
            copies.append(pltpu.make_async_copy(out_ref.at[:, pl.ds(at, LANES)], to, sems.at[n * hf + q]))
            copies[-1].start()
    for copy in copies:
        copy.wait()


def gather_kernel(steps, flag_ref, acc_ref, in_ref, after_ref, out_ref, east_ref, west_ref):
    count, ty, tx = out_ref.shape
    hf = count // steps
    acc = acc_ref[...].astype(BF16)
    for i in range(count):
        high, low = halves(in_ref[:, i * LANES : (i + 1) * LANES])
        total = bf_dot(acc, high) + bf_dot(acc, low)
        for l in range(tx // LANES):
            out_ref[i, :, l * LANES : (l + 1) * LANES] = total[l * ty : (l + 1) * ty]
    todo = late_fields(steps, 2 * hf)

    def read(f, l):
        n, q = todo[f]
        return out_ref[n * hf + q, :, l * LANES : (l + 1) * LANES] if q < hf else jnp.zeros((ty, LANES), F32)

    store_columns(read, len(todo), tx, steps, east_ref, west_ref, 0)

    @pl.when(flag_ref[0] != 0)
    def _():
        for ref in (east_ref, west_ref):
            ref[...] = pltpu.roll(ref[...], hf * steps, 1)


def forced_reader(steps, fields, flag_ref, send_ref, got_ref, keep_ref):
    count = (steps + 1) * (fields // 2)
    forced = (steps - 1) * fields

    def read(f, rows, cols):
        if f < 2 * forced:
            part, f = divmod(f, forced)
            return (send_ref, got_ref)[part][count + 2 + fields + f, rows, cols]
        if f == 2 * forced:
            return send_ref[count + 1, rows, cols]
        return jnp.where(flag_ref[0] == 0, keep_ref[count + 1, rows, cols], 1.0)

    return read, 2 * forced + 2


def state_rows_kernel(
    steps, fields, start, blocks, flag_ref, adj_hbm, send_ref, got_ref, keep_ref, west_ref, east_ref,
    north_ref, south_ref, edges, sems,
):
    _, nc, ty, tx = adj_hbm.shape
    copies = [
        pltpu.make_async_copy(adj_hbm.at[0, :, pl.ds(t, SUB), :], edges.at[i], sems.at[i])
        for i, t in enumerate((0, ty - SUB))
    ]
    for copy in copies:
        copy.start()
    forced, total = forced_reader(steps, fields, flag_ref, send_ref, got_ref, keep_ref)
    packed, _ = packed_reader(west_ref, east_ref, start, blocks, tx)
    for copy in copies:
        copy.wait()

    def read(f, t):
        if f < total:
            return forced(f, slice(t * SUB, (t + 1) * SUB), slice(0, tx))
        f -= total
        return edges[min(t, 1), f] if f < nc else packed(f - nc, t)

    widths = with_packed(state_widths(steps, fields, nc), blocks, tx, steps)
    send_rows(read, widths, ty, north_ref, south_ref)


def matrices_kernel(steps, fields, flag_ref, mix_ref, coup_ref, mix8_ref, coup8_ref, late_ref):
    nc = mix_ref.shape[1]
    ident = lax.broadcasted_iota(jnp.int32, (nc, nc), 0) == lax.broadcasted_iota(jnp.int32, (nc, nc), 1)
    step_m = mix_ref[0].T + ident.astype(F32)
    coup = coup_ref[0].T
    late = coup[:, fields:]
    powers = []
    for i in range(steps):
        powers.append(late)
        late = full_dot(step_m, late)
    at = 0
    for k in range(steps - 1, -1, -1):
        for j in range(k + 1):
            late_ref[:, at : at + fields * SUB] = grown(math.comb(k, j) * powers[k - j])
            at += fields * SUB
    first = lax.broadcasted_iota(jnp.int32, coup.shape, 1) < fields
    mix8_ref[...] = grown(step_m)
    coup8_ref[...] = grown(jnp.where(jnp.logical_or(first, flag_ref[0] == 0), coup, 0.0))


def mixed(state, force, spread, mix8, coup8, k, places):
    nc = state.shape[0]
    spots = [(slice(g * SUB, (g + 1) * SUB), slice(c, c + w)) for g, c, w in places]
    u = jnp.concatenate([state[:, rs, cs].reshape(nc * SUB, -1) for rs, cs in spots], axis=1)
    h = jnp.concatenate([force[k, :, rs, cs].reshape(coup8.shape[1] // 3, -1) for rs, cs in spots], axis=1)
    new = dot3(mix8, halves(u)) + bf_dot(coup8, stacked_columns(h))
    out, at = [], 0
    for (rs, cs), (_, _, w) in zip(spots, places):
        out.append((rs, cs, new[:, at : at + w].reshape(nc, SUB, w) + spread[:, rs, cs]))
        at += w
    return out


def side_places(groups, tx):
    per = tx // LANES
    return [tuple((g, tx, LANES) for g in range(at, min(at + per, groups))) for at in range(0, groups, per)]


def state_first_kernel(
    steps, fields, start, flag_ref, adj_hbm, send_ref, got_ref, keep_ref, west_ref, east_ref, mix8_ref, coup8_ref,
    new_ref, force_ref, ends_ref, adj_ref, state, spread, sem,
):
    nc, ty, tx = adj_ref.shape
    copy = pltpu.make_async_copy(adj_hbm.at[0], adj_ref, sem)
    copy.start()
    hw = steps
    per = LANES // hw
    read, total = forced_reader(steps, fields, flag_ref, send_ref, got_ref, keep_ref)

    def side(f, block):
        at = slice((start + block + f // per) * LANES, (start + block + f // per + 1) * LANES)
        return side_block(west_ref[:, at], east_ref[:, at], f, hw)

    def ext(f):
        return jnp.concatenate([read(f, slice(0, ty), slice(0, tx)), side(f, 0)], axis=1)

    forced = (steps - 1) * fields
    for k in range(1, steps):
        for q in range(fields):
            force_ref[k, q] = ext((k - 1) * fields + q)
            force_ref[k, fields + q] = ext(forced + (k - 1) * fields + q)
    at = (steps + 1) * (fields // 2) + 2
    for q in range(fields):
        force_ref[0, q, :, :tx] = send_ref[at + q]
        force_ref[0, fields + q, :, :tx] = got_ref[at + q]
    diff, wet = ext(2 * forced), ext(2 * forced + 1)
    mix8, coup8 = halves(mix8_ref[...]), stacked_rows(coup8_ref[...])
    block = -(-total // per)
    empty = jnp.zeros((SUB, tx + LANES), F32)
    copy.wait()
    for c in range(nc):
        u = wet * jnp.concatenate([adj_ref[c], side(c, block)], axis=1)
        state[c] = u
        p = diff * u
        spread[c] = ring_lap(jnp.concatenate([p, empty], axis=0))[:ty]
        ends_ref[c, :SUB] = p[:SUB]
        ends_ref[c, SUB:] = p[ty - SUB :]
    groups = ty // SUB
    for places in [((g, 0, tx),) for g in range(groups)] + side_places(groups, tx):
        for rs, cs, value in mixed(state, force_ref, spread, mix8, coup8, steps - 1, places):
            new_ref[:, rs, cs] = value


def state_kernel(
    steps, fields, start, blocks, flag_ref, new_ref, most_ref, ends_ref, send_ref, got_ref, keep_ref, west_ref,
    east_ref, north_ref, south_ref, mix8_ref, coup8_ref, out_hbm, ring_ref, out_ref, state, force, spread, sems,
):
    nc, ty, tx = new_ref.shape[0], new_ref.shape[1], new_ref.shape[2] - LANES
    hw = steps
    per = LANES // hw
    read, total = forced_reader(steps, fields, flag_ref, send_ref, got_ref, keep_ref)
    edge = edge_reader(north_ref, south_ref, with_packed(state_widths(steps, fields, nc), blocks, tx, hw))
    wests, easts = sides_with_rows(west_ref, east_ref, edge, total + nc, start, blocks, tx)

    def ext(f):
        main = read(f, slice(0, ty), slice(0, tx))
        return with_ring(main, wests[f // per], easts[f // per], f, edge, hw)

    def bottom(f, place, block):
        west, east = wests[block + place // per], easts[block + place // per]
        return jnp.concatenate([edge(f), side_block(west[ty:], east[ty:], place, hw)], axis=1)

    forced = (steps - 1) * fields
    for k in range(steps):
        force[k, :, :ty, :] = most_ref[k]
    for k in range(1, steps):
        for q in range(fields):
            for f, to in (((k - 1) * fields + q, q), (forced + (k - 1) * fields + q, fields + q)):
                force[k, to, ty:, :] = bottom(f, f, 0)
    diff, wet = ext(2 * forced), ext(2 * forced + 1)
    ring_ref[...] = diff
    mix8, coup8 = halves(mix8_ref[...]), stacked_rows(coup8_ref[...])
    block = -(-total // per)
    groups = ty // SUB
    main = [((g, 0, tx),) for g in range(groups)]
    below = [((groups, 0, tx),), ((groups, tx, LANES),)]

    sub = lax.broadcasted_iota(jnp.int32, (SUB, tx + LANES), 0)
    for c in range(nc):
        u = wet[ty:] * bottom(total + c, c, block)
        p = diff[ty:] * u
        stack = jnp.concatenate([ends_ref[c, SUB:], p, ends_ref[c, :SUB]], axis=0)
        spread[c, ty:, :] = ring_lap(stack)[SUB : 2 * SUB]
        state[c, ty:, :] = u
        state[c, :SUB, :] = new_ref[c, :SUB] + jnp.where(sub == 0, turn(p, 1), 0.0)
        state[c, SUB : ty - SUB, :] = new_ref[c, SUB : ty - SUB]
        state[c, ty - SUB : ty, :] = new_ref[c, ty - SUB :] + jnp.where(sub == SUB - 1, turn(p, -1), 0.0)
    for places in below:
        for rs, cs, value in mixed(state, force, spread, mix8, coup8, steps - 1, places):
            state[:, rs, cs] = value

    leaving = []
    for n in range(1, steps):
        k = steps - 1 - n
        small = n == steps - 1

        def one(c, carry):
            u = wet * state[c]
            state[c] = u
            spread[c] = ring_lap(diff * u)
            return carry

        lax.fori_loop(0, nc, one, 0, unroll=True)
        for places in main if small else main + below[:1] + side_places(groups + 1, tx):
            for rs, cs, value in mixed(state, force, spread, mix8, coup8, k, places):
                if small:
                    out_ref[:, rs, cs] = value
                else:
                    state[:, rs, cs] = value
            if small:
                leaving.append(pltpu.make_async_copy(out_ref.at[:, rs, :], out_hbm.at[:, rs, :], sems.at[len(leaving)]))
                leaving[-1].start()
    for copy in leaving:
        copy.wait()


def late_fields(steps, fields):
    return [(n, q) for n in range(steps - 1) for q in range(fields)]


def late_main(steps, hf, own_ref, far_ref):
    def read(n, q):
        return far_ref[n * hf + q] if q < hf else own_ref[n * hf + q - hf]

    return read


def late_rows_kernel(
    steps, blocks, own_ref, far_ref, west0_ref, west1_ref, east0_ref, east1_ref, north_ref, south_ref, west_ref, east_ref
):
    west_ref[...] = west0_ref[...] + west1_ref[...]
    east_ref[...] = east0_ref[...] + east1_ref[...]
    count, ty, tx = own_ref.shape
    hf = count // steps
    todo = late_fields(steps, 2 * hf)
    packed, _ = packed_reader(west_ref, east_ref, 0, blocks, tx)

    def read(f, t):
        if f >= len(todo):
            return packed(f - len(todo), t)
        n, q = todo[f]
        ref, i = (far_ref, n * hf + q) if q < hf else (own_ref, n * hf + q - hf)
        return ref[i, t * SUB : (t + 1) * SUB, :]

    send_rows(read, with_packed(late_widths(steps, 2 * hf), blocks, tx, steps), ty, north_ref, south_ref)


def late_kernel(
    steps, blocks, flag_ref, base_ref, ring_ref, late_ref, own_ref, far_ref, west_ref, east_ref, north_ref, south_ref,
    out_hbm, stack, out_ref, sems,
):
    count, ty, tx = own_ref.shape
    hf = count // steps
    fields = 2 * hf
    nc = base_ref.shape[0]
    per = LANES // steps
    todo = late_fields(steps, fields)
    read = late_main(steps, hf, own_ref, far_ref)

    @pl.when(flag_ref[0] == 0)
    def _():
        copy = pltpu.make_async_copy(base_ref, out_hbm.at[0], sems.at[0])
        copy.start()
        copy.wait()

    @pl.when(flag_ref[0] != 0)
    def _():
        diff = ring_ref[...]
        edge = edge_reader(north_ref, south_ref, with_packed(late_widths(steps, fields), blocks, tx, steps))
        wests, easts = sides_with_rows(west_ref, east_ref, edge, len(todo), 0, blocks, tx)
        at = 0
        for n in range(steps):
            k = steps - 1 - n
            for q in range(fields):
                r = read(n, q)
                if k:
                    f = todo.index((n, q))
                    r = with_ring(r, wests[f // per], easts[f // per], f, edge, steps)
                for j in range(k + 1):
                    stack[at + j * fields + q] = r[:ty, :tx]
                    if j < k:
                        r = ring_lap(diff * r)
            at += (k + 1) * fields
        big = halves(late_ref[...])
        copies = []
        for g in range(ty // SUB):
            rs = slice(g * SUB, (g + 1) * SUB)
            more = dot3(big, halves(stack[:, rs, :].reshape(-1, tx)))
            out_ref[:, rs, :] = base_ref[:, rs, :] + more.reshape(nc, SUB, tx)
            copies.append(pltpu.make_async_copy(out_ref.at[:, rs, :], out_hbm.at[0, :, rs, :], sems.at[g]))
            copies[-1].start()
        for copy in copies:
            copy.wait()


def shifted(x, axis, by, wrap, sects=None):
    size = lax.axis_size(axis)
    pairs = [(i, (i + by) % size) for i in range(size) if wrap or 0 <= i + by < size]
    if sects is None:
        return lax.ppermute(x, axis, pairs)
    a, b = sects
    return lax.ppermute(x, ("sect", axis), [(a * size + i, b * size + j) for i, j in pairs])


def struct(*shape):
    return jax.ShapeDtypeStruct(shape, F32)


def partial(kernel, *args):
    def run(*refs):
        kernel(*args, *refs)

    run.__name__ = kernel.__name__
    return run


def body(
    adjoint_init,
    diffusivity,
    mixing,
    coupling,
    history,
    extract,
    land_mask,
    regrid,
    atmos_tile_index,
    ocean_block_index,
    atmos_block_index,
):
    _, steps, fields, ty, tx = history.shape
    nc = adjoint_init.shape[1]
    hf, hw = fields // 2, steps
    per = LANES // hw
    sect = lax.axis_index("sect").astype(jnp.int32)
    tile = (lax.axis_index("gy") * lax.axis_size("gx") + lax.axis_index("gx")).astype(jnp.int32)
    flag = sect.reshape(1)
    tiles = lax.axis_size("gy") * lax.axis_size("gx")
    entries = ocean_block_index.shape[0] // tiles
    cap = 2 * entries // tiles
    cells = regrid.shape[1]
    slots = ty * tx // cells
    nb = tx // cells

    def exchange(x_after, x_before, axis, wrap, only=None):
        return shifted(x_after, axis, 1, wrap, only), shifted(x_before, axis, -1, wrap, only)

    count = (steps + 1) * hf
    coupling = jnp.swapaxes(coupling, 1, 2)
    columns = struct(ty, -(-nc // per) * LANES)
    keep, send, east, west = call(
        project_kernel,
        [struct(count + 2, ty, tx), struct(count + 2 + steps * fields, ty, tx), columns, columns],
        adjoint_init, land_mask, diffusivity, history, mixing, extract, coupling,
        hbm=tuple(range(7)),
        scratch=[
            pltpu.VMEM((nc, ty, tx), F32),
            pltpu.VMEM((ty, tx), jnp.int32),
            pltpu.VMEM(mixing.shape, F32),
            pltpu.VMEM(extract.shape, F32),
            pltpu.VMEM(coupling.shape, F32),
            pltpu.VMEM((-(-(steps + 1) * fields // SUB) * SUB, nc), F32),
            pltpu.SemaphoreType.DMA((6 + steps,)),
        ],
    )
    got = lax.ppermute(send, "sect", [(0, 1), (1, 0)])
    dest = atmos_tile_index.reshape(tiles, entries)
    sel, weights = call(
        partial(select_kernel, cap, slots, nb),
        [struct(tiles * cap, slots), struct(cells, cells)],
        tile.reshape(1), dest, ocean_block_index.reshape(tiles, entries), regrid,
        smem=(0,),
        hbm=(1, 2, 3),
        scratch=[pltpu.VMEM((tiles, entries), jnp.int32)] * 2 + [pltpu.SemaphoreType.DMA((3,))],
    )
    places, halo_count = field_places(steps, hf)
    blocks = -(-halo_count // per)
    total = 2 * (steps - 1) * fields + 2
    state_blocks = -(-total // per) + -(-nc // per)
    side = struct(ty, (blocks + state_blocks) * LANES)
    main, east, west = call(
        partial(force_kernel, places, halo_count, steps, fields),
        [struct(len(places), ty, tx), side, side],
        flag, keep, send, got, east, west, sel,
        smem=(0,),
    )
    from_west, from_east = exchange(east, west, "gx", True)
    widths = with_packed(projected_widths(places, halo_count, steps), blocks, tx, hw)
    north, south = call(
        partial(rows_kernel, widths, blocks),
        [struct(strip_places(widths)[1], SUB, tx)] * 2,
        main, from_west, from_east,
    )
    from_north, from_south = exchange(south, north, "gy", False)
    [packed] = call(
        partial(surface_kernel, places, halo_count, widths, steps, hf),
        [struct(tiles * cap, steps * hf * LANES)],
        main, from_west, from_east, from_north, from_south, weights, sel,
        hbm_out=(0,),
        scratch=[pltpu.VMEM((tiles * cap, steps * hf * LANES), F32), pltpu.SemaphoreType.DMA((steps * hf,))],
    )
    widths = with_packed(state_widths(steps, fields, nc), state_blocks, tx, hw)
    sizes = (steps, fields, blocks, state_blocks)
    north, south = call(
        partial(state_rows_kernel, *sizes),
        [struct(strip_places(widths)[1], SUB, tx)] * 2,
        flag, adjoint_init, send, got, keep, from_west, from_east,
        smem=(0,),
        hbm=(1,),
        scratch=[pltpu.VMEM((2, nc, SUB, tx), F32), pltpu.SemaphoreType.DMA((2,))],
    )
    packed, dest, mixing, north, south = lax.optimization_barrier((packed, dest, mixing, north, south))
    arrived = lax.all_to_all(
        packed.reshape(tiles, cap, -1), ("gy", "gx"), split_axis=0, concat_axis=0, tiled=True
    ).reshape(tiles * cap, -1)

    from_north, from_south = exchange(south, north, "gy", False)
    terms = fields * steps * (steps + 1) // 2
    ext = (ty + SUB, tx + LANES)
    mix8, coup8, late = call(
        partial(matrices_kernel, steps, fields),
        [struct(nc * SUB, nc * SUB), struct(nc * SUB, 2 * fields * SUB), struct(nc * SUB, terms * SUB)],
        flag, mixing, coupling,
        smem=(0,),
    )
    new, most, ends = call(
        partial(state_first_kernel, steps, fields, blocks),
        [struct(nc, ty, ext[1]), struct(steps, 2 * fields, ty, ext[1]), struct(nc, 2 * SUB, ext[1])],
        flag, adjoint_init, send, got, keep, from_west, from_east, mix8, coup8,
        smem=(0,),
        hbm=(1,),
        scratch=[
            pltpu.VMEM((nc, ty, tx), F32),
            pltpu.VMEM((nc, ty, ext[1]), F32),
            pltpu.VMEM((nc, ty, ext[1]), F32),
            pltpu.SemaphoreType.DMA,
        ],
    )
    base, ring = call(
        partial(state_kernel, *sizes),
        [struct(nc, ty, tx), struct(*ext)],
        flag, new, most, ends, send, got, keep, from_west, from_east, from_north, from_south, mix8, coup8,
        smem=(0,),
        hbm_out=(0,),
        scratch=[
            pltpu.VMEM((nc, ty, tx), F32),
            pltpu.VMEM((nc, *ext), F32),
            pltpu.VMEM((steps, 2 * fields, *ext), F32),
            pltpu.VMEM((nc, *ext), F32),
            pltpu.SemaphoreType.DMA((ty // SUB,)),
        ],
    )

    [acc] = call(
        partial(arrival_kernel, cap, slots, nb),
        [struct(slots, tiles * cap)],
        tile.reshape(1), dest, atmos_block_index.reshape(tiles, entries),
        smem=(0,),
    )
    halo_count = (steps - 1) * fields
    blocks = -(-halo_count // per)
    side = struct(ty, blocks * LANES)
    own, east, west = call(
        partial(gather_kernel, steps), [struct(steps * hf, ty, tx), side, side], flag, acc, arrived, ring, smem=(0,)
    )
    far = lax.ppermute(own, "sect", [(0, 1)])
    west1, east1 = exchange(east, west, "gx", True, (1, 1))
    west0, east0 = exchange(east, west, "gx", True, (0, 1))
    widths = with_packed(late_widths(steps, fields), blocks, tx, hw)
    rows = struct(strip_places(widths)[1], SUB, tx)
    north, south, from_west, from_east = call(
        partial(late_rows_kernel, steps, blocks), [rows, rows, side, side], own, far, west0, west1, east0, east1
    )
    from_north, from_south = exchange(south, north, "gy", False, (1, 1))
    [out] = call(
        partial(late_kernel, steps, blocks),
        [struct(1, nc, ty, tx)],
        flag, base, ring, late, own, far, from_west, from_east, from_north, from_south,
        smem=(0,),
        hbm_out=(0,),
        scratch=[
            pltpu.VMEM((terms, ty, tx), F32),
            pltpu.VMEM((nc, ty, tx), F32),
            pltpu.SemaphoreType.DMA((ty // SUB,)),
        ],
    )
    return out


def solution(mesh):
    placed = (
        P("sect", None, "gy", "gx"),
        P("sect", "gy", "gx"),
        P("sect", None, None),
        P("sect", None, None),
        P("sect", None, None, "gy", "gx"),
        P(),
        P("gy", "gx"),
        P(("gy", "gx"), None, None),
        P(),
        P(),
        P(),
    )
    return jax.shard_map(
        body, mesh=mesh, in_specs=placed, out_specs=P("sect", None, "gy", "gx"), check_vma=False
    )
```
